32 devices in a mesh: rec: 2 (over x), tm: 16 (over z, y, core).
Axes of the slice: x: 2, y: 2, z: 4, core: 2. Of those that a mesh axis runs over, the one named last changes fastest.
Arguments:
- raw: bfloat16 [2048, 6144], P(('rec', 'tm')), parts along dimension 0, may hold values from -8.5 to 8.5
- pole: float32 [6144], replicated, may hold values from 0.96 to 1, as said below
- order: int32 [96, 64], replicated, may hold values from 0 to 63, each once within a row
- templates: bfloat16 [1152, 61, 32], replicated, may hold values from -0.125 to 0.125
- support: int32 [1152, 32], replicated, may hold values 0 or 1
Outputs:
- scores: bfloat16 [2048, 1152], P(('rec', 'tm')), parts along dimension 0
- whitening: float32 [384, 32, 32], P('rec'), parts along dimension 0
The draws below stay inside these ranges and needn't reach their ends.
There are 2 independent parts, one for each index of `rec`. The reference program is written for one: setup_inputs(seed, part) draws one part's arguments, and reference() takes and returns one part's arrays. A program takes and returns all parts, laid end to end along the dimension named above; an argument that names none is the same for every part. Nothing has to cross between parts.
Inputs may be any that keep to these rules, and one draw needn't show every extreme that they name: Each channel's pole lies in this range. Each row of order is a permutation of 0 to 63.
All inputs are finite; a program needn't handle non-finite values.
Results may differ from the reference program's by a relative error of at most 0.0075.
Values may be sent and summed in bfloat16 or wider, within the bound.
No kernel may reach another device: no remote copies, remote signals or barrier semaphores. Data moves between devices by JAX's collectives and lax.ppermute only.
A program may use at most 128 MiB of HBM per device.

```python
import math
import jax
import jax.numpy as jnp
from jax import lax

CHANNELS = 6144
NB = 32
TAPS = 61
NS_ITERS = 4
TS = 64
GROUPS = 192
TEMPLATES = 1152
TOTAL_T = 1024


def draw_raw(key, part):
    noise_key = jax.random.fold_in(key, 21)
    offset_key = jax.random.fold_in(key, 22)
    amp_key = jax.random.fold_in(key, 24)
    cycle_key = jax.random.fold_in(key, 25)
    phase_key = jax.random.fold_in(key, 26)
    noise = jnp.clip(jax.random.normal(noise_key, (TOTAL_T, CHANNELS), jnp.float32), -4.0, 4.0)
    offset = jax.random.uniform(offset_key, (CHANNELS,), jnp.float32, -3.0, 3.0)
    amplitude = jax.random.uniform(amp_key, (CHANNELS,), jnp.float32, 0.5, 1.5)
    cycles = jax.random.uniform(cycle_key, (CHANNELS,), jnp.float32, 0.2, 1.0)
    phase = jax.random.uniform(phase_key, (CHANNELS,), jnp.float32, -math.pi, math.pi)
    times = jnp.arange(TOTAL_T, dtype=jnp.float32) / TOTAL_T
    drift = amplitude[None] * jnp.sin(2.0 * math.pi * times[:, None] * cycles[None] + phase[None])
    return jnp.clip(noise + offset[None] + drift, -8.5, 8.5).astype(jnp.bfloat16)


def draw_pole(key, part):
    kind_key = jax.random.fold_in(key, 11)
    rate_key = jax.random.fold_in(key, 12)
    share = 0.5
    slow = jax.random.uniform(kind_key, (CHANNELS,), jnp.float32) < share
    spread = jax.random.uniform(rate_key, (CHANNELS,), jnp.float32)
    fast_rate = jnp.exp(math.log(1.0 / 50.0) + spread * (math.log(1.0 / 30.0) - math.log(1.0 / 50.0)))
    slow_rate = jnp.exp(math.log(0.05) + spread * (math.log(2.0) - math.log(0.05))) / TOTAL_T
    return (1.0 - jnp.where(slow, slow_rate, fast_rate)).astype(jnp.float32)


def place_ends(drawn, rng, smallest, largest):
    spot = [jax.random.randint(jax.random.fold_in(rng, axis), (), 0, length) for axis, length in enumerate(drawn.shape)]
    widest = drawn.shape.index(max(drawn.shape))
    next_to = spot[:widest] + [(spot[widest] + 1) % drawn.shape[widest]] + spot[widest + 1:]
    return drawn.at[tuple(spot)].set(smallest).at[tuple(next_to)].set(largest)


def bell_draw(own_key, extent, deviation, limit, held_as=jnp.bfloat16):
    return jnp.clip(deviation * jax.random.normal(own_key, extent, jnp.float32), -limit, limit).astype(held_as)


def setup_inputs(seed: int = 0, part: int = 0) -> dict:
    streams_of = jax.random.split(jax.random.key(seed), 6)
    own_keys = jax.random.split(jax.random.fold_in(streams_of[5], part), 6)
    raw = draw_raw(jax.random.fold_in(jax.random.fold_in(streams_of[5], part), 71), part)
    pole = draw_pole(jax.random.fold_in(streams_of[5], 71), part)
    order = jax.vmap(lambda own: jax.random.permutation(own, 64))(jax.random.split(streams_of[2], (CHANNELS // 64))).reshape((CHANNELS // 64, 64)).astype(jnp.int32)
    templates = bell_draw(streams_of[3], (TEMPLATES, TAPS, NB), (NB * TAPS) ** -0.5, 0.125)
    support = place_ends((jax.random.randint(streams_of[4], (TEMPLATES, NB), 0, 4) < 3).astype(jnp.int32), jax.random.fold_in(streams_of[4], 1), 0, 1)
    return dict(raw=raw, pole=pole, order=order, templates=templates, support=support)


RIDGE = 0.1

def compose(earlier, later):
    return (earlier[0] * later[0], earlier[1] * later[0] + later[1])

def root_inverse(covariance):
    width = covariance.shape[-1]
    identity = jnp.eye(width, dtype=jnp.float32)
    traces = jnp.trace(covariance, axis1=1, axis2=2)
    shifted = covariance + (RIDGE * traces / width)[:, None, None] * identity
    norms = jnp.sqrt(lax.optimization_barrier(jnp.sum(shifted * shifted, axis=(1, 2))))
    estimate = shifted / norms[:, None, None]
    inverse = jnp.broadcast_to(identity, shifted.shape)
    for repeat in range(NS_ITERS):
        middle = 1.5 * identity - 0.5 * jnp.einsum('gij,gjk->gik', inverse, estimate, precision=lax.Precision.HIGHEST)
        estimate = jnp.einsum('gij,gjk->gik', estimate, middle, precision=lax.Precision.HIGHEST)
        inverse = jnp.einsum('gij,gjk->gik', middle, inverse, precision=lax.Precision.HIGHEST)
    return inverse / jnp.sqrt(norms)[:, None, None]

def reference(raw, pole, order, templates, support):
    total_t = raw.shape[0]
    n_chan = raw.shape[1]
    channel_ids = (order + 64 * jnp.arange(order.shape[0], dtype=jnp.int32)[:, None]).reshape(-1).astype(jnp.int32)
    half_sum = 0.5 * (1.0 + pole)
    blocks = raw.reshape(total_t // TS, TS, n_chan)

    def advance(carry, raw_block):
        state, last_row, covariance = carry
        current = raw_block.astype(jnp.float32)
        earlier = jnp.concatenate([last_row[None], current[:-1]], axis=0)
        drive = half_sum * (current - earlier)
        drive = drive.at[0].add(pole * state)
        powers = jnp.broadcast_to(pole, drive.shape)
        unused, filtered = lax.associative_scan(compose, (powers, drive))
        stored = filtered.astype(jnp.bfloat16)
        grouped = stored[:, channel_ids].reshape(TS, GROUPS, NB).astype(jnp.float32)
        covariance = covariance + jnp.einsum('tgj,tgk->gjk', grouped, grouped, precision=lax.Precision.HIGHEST)
        return ((filtered[-1], current[-1], covariance), stored)
    start = (jnp.zeros((n_chan,), jnp.float32), jnp.zeros((n_chan,), jnp.float32), jnp.zeros((GROUPS, NB, NB), jnp.float32))
    final, stored_all = lax.scan(advance, start, blocks)
    covariance = final[2] / total_t
    whitening = root_inverse(covariance)
    grouped_all = stored_all.reshape(total_t, n_chan)[:, channel_ids].reshape(total_t, GROUPS, NB).astype(jnp.float32)
    whitened = jnp.einsum('tgk,gjk->tgj', grouped_all, whitening, precision=lax.Precision.HIGHEST).astype(jnp.bfloat16).reshape(total_t, n_chan)
    padded = jnp.concatenate([whitened, jnp.zeros((TAPS - 1, n_chan), jnp.bfloat16)], axis=0)[None].astype(jnp.float32)
    kernel = (templates.astype(jnp.float32) * support[:, None, :].astype(jnp.float32)).transpose(1, 2, 0)
    scores = lax.conv_general_dilated(padded, kernel, (1,), 'VALID', dimension_numbers=('NWC', 'WIO', 'NWC'), feature_group_count=GROUPS, precision=lax.Precision.HIGHEST)[0]
    return (scores.astype(jnp.bfloat16), whitening)
```

```python
import functools

import jax
import jax.numpy as jnp
from jax import lax
from jax.experimental import pallas as pl
from jax.experimental.pallas import tpu as pltpu
from jax.sharding import PartitionSpec as P

NB = 32
PACK = 4
LANES = NB * PACK
STEP = 8
NS_ITERS = 4
RIDGE = 0.1
VMEM_LIMIT = 28 * 1024 * 1024
F32, BF16 = jnp.float32, jnp.bfloat16


def nt_dot(a, b):
    return lax.dot_general(a, b, (((1,), (1,)), ((), ())), preferred_element_type=F32)


def halves(a):
    high = a.astype(BF16)
    return high, (a - high.astype(F32)).astype(BF16)


def mul(a, b):
    a_high, a_low = halves(a)
    b_high, b_low = halves(b)
    right = jnp.concatenate([b_high, b_low], axis=1)
    out = jnp.dot(
        jnp.concatenate([a_high, a_low], axis=1),
        jnp.concatenate([right, right], axis=0),
        preferred_element_type=F32,
    )
    return out[:, :LANES] + out[:, LANES:]


def down(v, distance):
    zeros = jnp.zeros((distance, v.shape[1]), v.dtype)
    return jnp.concatenate([zeros, v[:-distance]], axis=0)


def up(v):
    return jnp.concatenate([v[1:], jnp.zeros((1, v.shape[1]), v.dtype)], axis=0)


def prepare_kernel(
    groups, per, rows, mine, left_ref, right_ref, left_used, right_used, order_ref, pole_ref,
    weights_ref, picks_ref, poles_ref,
):
    taps = left_ref.shape[0]
    packs = weights_ref.shape[0]
    me = mine[0]
    count = groups * per
    size = packs * rows
    row = lax.broadcasted_iota(jnp.int32, (size, 2 * LANES), 0)
    lane = lax.broadcasted_iota(jnp.int32, (size, 2 * LANES), 1)
    number = (row // rows) * PACK * per + row % rows
    real = (row % rows < PACK * per) & (number < count)
    base = ((me * count) // LANES) * LANES
    select = (real & (base + lane == me * count + number)).astype(F32).astype(BF16)
    row = lax.broadcasted_iota(jnp.int32, (size, LANES), 0)
    lane = lax.broadcasted_iota(jnp.int32, (size, LANES), 1)
    own = (row % rows) // per == lane // NB
    used = jnp.concatenate([left_used[...], right_used[...]], axis=1).astype(F32).astype(BF16)
    pad = (STEP - 1) * rows
    for c in range(packs):
        weights_ref[c, :pad, :] = jnp.zeros((pad, LANES), BF16)
        weights_ref[c, pad + taps * rows:, :] = jnp.zeros((pad, LANES), BF16)
    for s in range(taps):
        block = jnp.concatenate([left_ref[s], right_ref[s]], axis=1) * used
        spread = nt_dot(select, jnp.concatenate([block] * PACK, axis=0))
        spread = jnp.where(own, spread, 0.0).astype(BF16)
        for c in range(packs):
            weights_ref[c, pad + s * rows:pad + (s + 1) * rows, :] = spread[c * rows:(c + 1) * rows]

    length, blocks = order_ref.shape
    lane = lax.broadcasted_iota(jnp.int32, (length, blocks), 1)
    ids_lane = lax.broadcasted_iota(jnp.int32, (LANES, LANES), 1)
    for c in range(packs):
        start = me * groups + PACK * c
        block = start // 2
        ids = jnp.concatenate(
            [
                jnp.sum(jnp.where(lane == block + k, order_ref[...], 0), axis=1, keepdims=True) + length * k
                for k in range(2)
            ],
            axis=0,
        )
        pole = pole_ref[pl.ds(block // 2, 1), :]
        if groups % PACK:
            last = pole_ref.shape[0] - 1
            after = pole_ref[pl.ds(jnp.minimum(block // 2 + 1, last), 1), :]
            joined = jnp.concatenate([pole[:, length:], after[:, :length]], axis=1)
            pole = jnp.where(block % 2 == 1, joined, pole)
            ids = jnp.where(start % 2 == 1, jnp.concatenate([ids[NB:], ids[:NB]], axis=0), ids)
        pick = (ids_lane == ids).astype(F32)
        picks_ref[c] = pick.astype(BF16)
        poles_ref[c] = lax.dot_general(
            jnp.broadcast_to(pole, (8, LANES)), pick, (((1,), (1,)), ((), ())),
            precision=lax.Precision.HIGHEST, preferred_element_type=F32,
        )


def main_kernel(
    groups, rows, taps, raw_any, picks_ref, poles_ref, weights_any, out_ref,
    raw_ref, weights_ref, first, state, stored, white, total, sems,
):
    n, length, width = raw_ref.shape
    fetch_raw = pltpu.make_async_copy(raw_any, raw_ref, sems.at[0])
    fetch_weights = pltpu.make_async_copy(weights_any, weights_ref, sems.at[1])
    fetch_raw.start()
    fetch_weights.start()
    packs = range(width // LANES)
    blocks = length // STEP
    row_id = lax.broadcasted_iota(jnp.int32, (LANES, LANES), 0)
    lane_id = lax.broadcasted_iota(jnp.int32, (LANES, LANES), 1)
    same = (row_id // NB) == (lane_id // NB)
    eye = (row_id == lane_id).astype(F32)
    ones = same.astype(F32)
    poles = [jnp.broadcast_to(poles_ref[c, :1, :], (n, LANES)) for c in packs]
    gains = [0.5 * (1.0 + pole) for pole in poles]
    fetch_raw.wait()
    for c in packs:
        part = raw_ref[:, :, c * LANES:(c + 1) * LANES].reshape(n * length, LANES)
        first[c] = nt_dot(part, picks_ref[c])

    level = [jnp.zeros((n, LANES), F32) for c in packs]
    last = [down(first[c, pl.ds(length - 1, n, stride=length), :], 1) for c in packs]
    for j in range(length):
        for c in packs:
            now = first[c, pl.ds(j, n, stride=length), :]
            level[c] = poles[c] * level[c] + gains[c] * (now - last[c])
            last[c] = now
            state[c, j * n:(j + 1) * n, :] = level[c]
    incoming = []
    for c in packs:
        span, square, left = None, poles[c], length
        while left:
            if left % 2:
                span = square if span is None else span * square
            square = square * square
            left //= 2
        value, distance = level[c], 1
        while distance < n:
            value = value + span * down(value, distance)
            span = span * span
            distance *= 2
        incoming.append(down(value, 1))
    carried = list(incoming)
    for j in range(length):
        for c in packs:
            carried[c] = carried[c] * poles[c]
            stored[c, j * n:(j + 1) * n, :] = (state[c, j * n:(j + 1) * n, :] + carried[c]).astype(BF16)

    estimate, inverse, norms = [], [], []
    for c in packs:
        y = stored[c]
        gram = lax.dot_general(y, y, (((0,), (0,)), ((), ())), preferred_element_type=F32)
        cov = jnp.where(same, gram / (n * length), 0.0)
        sums = jnp.concatenate(
            [jnp.sum(cov * eye, axis=0, keepdims=True), jnp.sum(cov * cov, axis=0, keepdims=True),
             jnp.zeros((6, LANES), F32)], axis=0,
        )
        sums = jnp.dot(sums, ones, precision=lax.Precision.HIGHEST, preferred_element_type=F32)
        trace, squares = sums[0:1], sums[1:2]
        ridge = RIDGE * trace / NB
        norm = jnp.sqrt(squares + 2.0 * ridge * trace + NB * ridge * ridge)
        norms.append(norm)
        estimate.append((cov + ridge * eye) / norm)
    for repeat in range(NS_ITERS):
        if repeat == 0:
            middle = [1.5 * eye - 0.5 * estimate[c] for c in packs]
        else:
            middle = [1.5 * eye - 0.5 * mul(inverse[c], estimate[c]) for c in packs]
        if repeat < NS_ITERS - 1:
            estimate = [mul(estimate[c], middle[c]) for c in packs]
        inverse = middle if repeat == 0 else [mul(middle[c], inverse[c]) for c in packs]

    base = len(packs) * 2 * blocks
    tile = LANES // NB
    fold = ((row_id % NB) == (lane_id % NB)).astype(F32).astype(BF16)
    spread = []
    whitenings = [inverse[c] / jnp.sqrt(norms[c]) for c in packs]
    for c in packs:
        wide = jnp.dot(whitenings[c].astype(BF16), fold, preferred_element_type=F32)
        spread.append(jnp.where(lane_id // NB == row_id % tile, wide, 0.0).astype(BF16))
    tiles = NB // tile
    held = len(packs) * PACK
    to = lax.broadcasted_iota(jnp.int32, (tiles * held, held * NB), 0)
    source = lax.broadcasted_iota(jnp.int32, (tiles * held, held * NB), 1)
    gather = (source // NB == to % held) & ((source % NB) // tile == to // held)
    flat = jnp.dot(
        gather.astype(F32).astype(BF16), jnp.concatenate(spread, axis=0), preferred_element_type=F32
    ).astype(BF16)
    for seg in range(n):
        out_ref[seg, base:base + tiles * held, :] = flat
    for c in packs:
        whitening = whitenings[c]
        right = jnp.concatenate(halves(whitening), axis=1)
        for i in range(blocks):
            y = stored[c, i * STEP * n:(i + 1) * STEP * n, :]
            rows_white = nt_dot(jnp.concatenate([y, y], axis=1), right)
            for b in range(STEP):
                w = rows_white[b * n:(b + 1) * n]
                white[c, b, i * n:(i + 1) * n, :] = w.astype(BF16)
                white[c, b, (blocks + i) * n:(blocks + i + 1) * n, :] = up(w).astype(BF16)

    reach = taps + STEP - 1
    fetch_weights.wait()
    size = blocks * n
    for c in packs:
        acc = jnp.zeros((size, STEP * rows), F32)
        for u in range(0, reach, 2):
            pair = [u] if u + 1 == reach else [u, u + 1]
            acc = acc + nt_dot(
                jnp.concatenate(
                    [white[c, v % STEP, (v // STEP) * n:(v // STEP) * n + size, :] for v in pair], axis=1
                ),
                jnp.concatenate(
                    [weights_ref[c, v * rows:(v + STEP) * rows, :] for v in pair], axis=1
                ),
            )
        total[0] = acc[:, :LANES]
        total[1] = acc[:, LANES:]
        for seg in range(n):
            both = [total[h, pl.ds(seg, blocks, stride=n), :] for h in range(2)]
            out_ref[seg, c * 2 * blocks:(c + 1) * 2 * blocks, :] = jnp.concatenate(both, axis=0).astype(BF16)


def final_kernel(groups, per, rows, got_ref, scores_ref, whitening_ref, joined, wide):
    n = got_ref.shape[0]
    packs = -(-groups // PACK)
    length, columns = scores_ref.shape
    blocks = length // STEP
    base = packs * 2 * blocks
    held = packs * PACK
    tiles = (NB * NB) // LANES
    for src in range(n):
        for k in range(tiles):
            at = base + k * held
            block = got_ref[src, base:base + tiles * held, :].astype(F32) if k == 0 else block
            joined[src * groups:(src + 1) * groups, k * LANES:(k + 1) * LANES] = (
                block[k * held:k * held + groups]
            )
    step = 2 * LANES
    row_id = lax.broadcasted_iota(jnp.int32, (step, step), 0)
    lane_id = lax.broadcasted_iota(jnp.int32, (step, step), 1)
    eye = (row_id == lane_id).astype(F32).astype(BF16)
    high = step // NB
    for k in range((NB * NB) // step):
        turned = nt_dot(eye, joined[:, k * step:(k + 1) * step].astype(BF16))
        whitening_ref[k * high:(k + 1) * high] = turned.reshape(high, NB, n * groups)
    each = min(PACK, groups) * per
    lane = lax.broadcasted_iota(jnp.int32, (blocks, LANES), 1)
    pieces = [(src, c) for src in range(n) for c in range(packs)]
    tiles = columns // LANES
    for h in range(2):
        loaded = {}
        for o in range(tiles):
            outs = [None] * (STEP // 2)
            for m in range((o * LANES) // each, min(len(pieces), -(-((o + 1) * LANES) // each))):
                if m not in loaded:
                    src, c = pieces[m]
                    loaded[m] = got_ref[src, c * 2 * blocks:(c + 1) * 2 * blocks, :].astype(F32)[
                        h * blocks:(h + 1) * blocks
                    ]
                at = m * each - o * LANES
                for q in range(STEP // 2):
                    shift = (at - q * rows) % LANES
                    moved = pltpu.roll(loaded[m], shift, 1) if shift else loaded[m]
                    if outs[q] is None:
                        outs[q] = moved
                    else:
                        outs[q] = jnp.where(lane >= at, moved, outs[q])
            for q in range(STEP // 2):
                tb = STEP - 1 - (h * (STEP // 2) + q)
                wide[o, pl.ds(tb, blocks, stride=STEP), :] = outs[q]
    for o in range(tiles):
        scores_ref[:, o * LANES:(o + 1) * LANES] = wide[o].astype(BF16)


def params():
    return pltpu.CompilerParams(vmem_limit_bytes=VMEM_LIMIT)


def local(raw, pole, order, templates, support):
    length, channels = raw.shape
    n = lax.axis_size("tm")
    me = lax.axis_index("tm").astype(jnp.int32).reshape(1)
    all_groups = channels // NB
    groups = all_groups // n
    per = templates.shape[0] // all_groups
    taps = templates.shape[1]
    count = groups * per
    packs = -(-groups // PACK)
    rows = NB
    width = packs * LANES
    blocks = length // STEP

    if groups % PACK == 0:
        send = raw.reshape(length, n, width).transpose(1, 0, 2)
    else:
        pieces = [raw[:, (d * groups // 2) * 2 * NB:][:, :width] for d in range(n)]
        send = jnp.stack(pieces, axis=0)
    received = lax.all_to_all(send, "tm", 0, 0, tiled=True)

    vmem = pl.BlockSpec(memory_space=pltpu.VMEM)
    anywhere = pl.BlockSpec(memory_space=pl.ANY)
    tap_rows = (taps + 2 * (STEP - 1)) * rows
    by_lane = templates.transpose(1, 2, 0)
    used = support.T
    ends = by_lane.shape[2] // LANES - 1

    def left(s):
        return (s[0] * count) // LANES

    def right(s):
        return jnp.minimum((s[0] * count) // LANES + 1, ends)

    def whole(shape):
        return pl.BlockSpec(shape, lambda i, s: (0,) * len(shape))

    poles = pole.reshape(-1, LANES)
    shapes = [
        jax.ShapeDtypeStruct((packs, tap_rows, LANES), BF16),
        jax.ShapeDtypeStruct((packs, LANES, LANES), BF16),
        jax.ShapeDtypeStruct((packs, 8, LANES), F32),
    ]
    weights, picks, permuted = pl.pallas_call(
        functools.partial(prepare_kernel, groups, per, rows),
        out_shape=shapes,
        grid_spec=pltpu.PrefetchScalarGridSpec(
            num_scalar_prefetch=1,
            grid=(1,),
            in_specs=[
                pl.BlockSpec((taps, NB, LANES), lambda i, s: (0, 0, left(s))),
                pl.BlockSpec((taps, NB, LANES), lambda i, s: (0, 0, right(s))),
                pl.BlockSpec((NB, LANES), lambda i, s: (0, left(s))),
                pl.BlockSpec((NB, LANES), lambda i, s: (0, right(s))),
                whole(order.T.shape),
                whole(poles.shape),
            ],
            out_specs=[whole(shape.shape) for shape in shapes],
        ),
        compiler_params=params(),
        name="prepare",
    )(me, by_lane, by_lane, used, used, order.T, poles)

    total_rows = n * length
    payload = jax.ShapeDtypeStruct((n, packs * (2 * blocks + NB), LANES), BF16)
    sent = pl.pallas_call(
        functools.partial(main_kernel, groups, rows, taps),
        out_shape=payload,
        in_specs=[anywhere, vmem, vmem, anywhere],
        out_specs=vmem,
        scratch_shapes=[
            pltpu.VMEM((n, length, width), BF16),
            pltpu.VMEM((packs, tap_rows, LANES), BF16),
            pltpu.VMEM((packs, total_rows, LANES), F32),
            pltpu.VMEM((packs, total_rows, LANES), F32),
            pltpu.VMEM((packs, total_rows, LANES), BF16),
            pltpu.VMEM((packs, STEP, 2 * blocks * n, LANES), BF16),
            pltpu.VMEM((2, blocks * n, LANES), F32),
            pltpu.SemaphoreType.DMA((2,)),
        ],
        compiler_params=params(),
        name="filter_whiten_match",
    )(received, picks, permuted, weights)
    got = lax.all_to_all(sent, "tm", 0, 0, tiled=True)

    columns = all_groups * per
    scores, whitening = pl.pallas_call(
        functools.partial(final_kernel, groups, per, rows),
        out_shape=[
            jax.ShapeDtypeStruct((length, columns), BF16),
            jax.ShapeDtypeStruct((NB, NB, all_groups), F32),
        ],
        in_specs=[vmem],
        out_specs=[vmem, vmem],
        scratch_shapes=[
            pltpu.VMEM((all_groups, NB * NB), F32),
            pltpu.VMEM((columns // LANES, length, LANES), F32),
        ],
        compiler_params=params(),
        name="unpack",
    )(got)
    return scores, whitening.transpose(2, 0, 1)


def solution(mesh):
    in_specs = (P(("rec", "tm"), None), P(), P(), P(), P())
    out_specs = (P(("rec", "tm"), None), P("rec", None, None))
    return jax.shard_map(local, mesh=mesh, in_specs=in_specs, out_specs=out_specs, check_vma=False)
```

```python
import functools

import jax
import jax.numpy as jnp
from jax import lax
from jax.experimental import pallas as pl
from jax.experimental.pallas import tpu as pltpu
from jax.sharding import PartitionSpec as P

NB = 32
PACK = 4
LANES = NB * PACK
STEP = 8
NS_ITERS = 4
RIDGE = 0.1
MIB = 1024 * 1024
F32, BF16 = jnp.float32, jnp.bfloat16


def nt_dot(a, b):
    return lax.dot_general(a, b, (((1,), (1,)), ((), ())), preferred_element_type=F32)


def halves(a):
    high = a.astype(BF16)
    return high, (a - high.astype(F32)).astype(BF16)


def mul(a, b):
    a_high, a_low = halves(a)
    b_high, b_low = halves(b)
    right = jnp.concatenate([b_high, b_low], axis=1)
    out = jnp.dot(
        jnp.concatenate([a_high, a_low], axis=1),
        jnp.concatenate([right, right], axis=0),
        preferred_element_type=F32,
    )
    return out[:, :LANES] + out[:, LANES:]


def down(v, distance):
    zeros = jnp.zeros((distance, v.shape[1]), v.dtype)
    return jnp.concatenate([zeros, v[:-distance]], axis=0)


def up(v):
    return jnp.concatenate([v[1:], jnp.zeros((1, v.shape[1]), v.dtype)], axis=0)


def template_kernel(
    groups, per, rows, mine, left_ref, right_ref, left_used, right_used, weights_ref, lined
):
    taps = left_ref.shape[0]
    packs = weights_ref.shape[0]
    me = mine[0]
    count = groups * per
    lane = lax.broadcasted_iota(jnp.int32, (2 * LANES, packs * LANES), 1)
    row = lax.broadcasted_iota(jnp.int32, (2 * LANES, packs * LANES), 0)
    number = (lane // LANES) * PACK * per + lane % rows
    real = (lane % rows < PACK * per) & (number < count)
    base = ((me * count) // LANES) * LANES
    select = (real & (base + row == me * count + number)).astype(F32).astype(BF16)
    used = jnp.concatenate([left_used[...], right_used[...]], axis=1).astype(F32).astype(BF16)
    pad = (STEP - 1) * NB
    lined[:pad, :] = jnp.zeros((pad, packs * LANES), BF16)
    lined[pad + taps * NB:, :] = jnp.zeros((pad, packs * LANES), BF16)
    for s in range(0, taps, STEP):
        group = range(s, min(taps, s + STEP))
        blocks = [jnp.concatenate([left_ref[t], right_ref[t]], axis=1) * used for t in group]
        picked = jnp.dot(jnp.concatenate(blocks, axis=0), select, preferred_element_type=F32)
        lined[pad + s * NB:pad + (s + len(group)) * NB, :] = picked.astype(BF16)
    lane = lax.broadcasted_iota(jnp.int32, (NB, LANES), 1)
    taken = [(lane // rows == k).astype(F32).astype(BF16) for k in range(LANES // rows)]
    owned = [((lane % rows) // per == g).astype(F32).astype(BF16) for g in range(PACK)]
    for v in range(weights_ref.shape[1] // LANES):
        for c in range(packs):
            block = sum(
                lined[(v + k) * NB:(v + k + 1) * NB, c * LANES:(c + 1) * LANES] * taken[k]
                for k in range(LANES // rows)
            )
            for g in range(PACK):
                weights_ref[c, v * LANES + g * NB:v * LANES + (g + 1) * NB, :] = block * owned[g]


def order_kernel(groups, mine, order_ref, pole_ref, picks_ref, poles_ref):
    me = mine[0]
    packs = picks_ref.shape[0]
    length, blocks = order_ref.shape
    lane = lax.broadcasted_iota(jnp.int32, (length, blocks), 1)
    ids_lane = lax.broadcasted_iota(jnp.int32, (LANES, LANES), 1)
    for c in range(packs):
        start = me * groups + PACK * c
        block = start // 2
        ids = jnp.concatenate(
            [
                jnp.sum(jnp.where(lane == block + k, order_ref[...], 0), axis=1, keepdims=True) + length * k
                for k in range(2)
            ],
            axis=0,
        )
        pole = pole_ref[pl.ds(block // 2, 1), :]
        if groups % PACK:
            last = pole_ref.shape[0] - 1
            after = pole_ref[pl.ds(jnp.minimum(block // 2 + 1, last), 1), :]
            joined = jnp.concatenate([pole[:, length:], after[:, :length]], axis=1)
            pole = jnp.where(block % 2 == 1, joined, pole)
            ids = jnp.where(start % 2 == 1, jnp.concatenate([ids[NB:], ids[:NB]], axis=0), ids)
        pick = (ids_lane == ids).astype(F32)
        picks_ref[c] = pick.astype(BF16)
        poles_ref[c] = lax.dot_general(
            jnp.broadcast_to(pole, (8, LANES)), pick, (((1,), (1,)), ((), ())),
            precision=lax.Precision.HIGHEST, preferred_element_type=F32,
        )


def main_kernel(
    groups, rows, taps, raw_any, picks_ref, poles_ref, weights_any, out_ref,
    raw_ref, weights_ref, first, state, stored, white, total, sems,
):
    n, length, width = raw_ref.shape
    fetch_raw = pltpu.make_async_copy(raw_any, raw_ref, sems.at[0])
    fetch_weights = pltpu.make_async_copy(weights_any, weights_ref, sems.at[1])
    fetch_raw.start()
    packs = range(width // LANES)
    blocks = length // STEP
    row_id = lax.broadcasted_iota(jnp.int32, (LANES, LANES), 0)
    lane_id = lax.broadcasted_iota(jnp.int32, (LANES, LANES), 1)
    same = (row_id // NB) == (lane_id // NB)
    eye = (row_id == lane_id).astype(F32)
    ones = same.astype(F32)
    poles = [jnp.broadcast_to(poles_ref[c, :1, :], (n, LANES)) for c in packs]
    gains = [0.5 * (1.0 + pole) for pole in poles]
    fetch_raw.wait()
    fetch_weights.start()
    for c in packs:
        part = raw_ref[:, :, c * LANES:(c + 1) * LANES].reshape(n * length, LANES)
        first[c] = nt_dot(part, picks_ref[c])

    level = [jnp.zeros((n, LANES), F32) for c in packs]
    last = [down(first[c, pl.ds(length - 1, n, stride=length), :], 1) for c in packs]
    for j in range(length):
        for c in packs:
            now = first[c, pl.ds(j, n, stride=length), :]
            level[c] = poles[c] * level[c] + gains[c] * (now - last[c])
            last[c] = now
            state[c, j * n:(j + 1) * n, :] = level[c]
    incoming = []
    for c in packs:
        span, square, left = None, poles[c], length
        while left:
            if left % 2:
                span = square if span is None else span * square
            square = square * square
            left //= 2
        value, distance = level[c], 1
        while distance < n:
            value = value + span * down(value, distance)
            span = span * span
            distance *= 2
        incoming.append(down(value, 1))
    carried = list(incoming)
    for j in range(length):
        for c in packs:
            carried[c] = carried[c] * poles[c]
            stored[c, j * n:(j + 1) * n, :] = (state[c, j * n:(j + 1) * n, :] + carried[c]).astype(BF16)

    estimate, inverse, norms = [], [], []
    for c in packs:
        y = stored[c]
        gram = lax.dot_general(y, y, (((0,), (0,)), ((), ())), preferred_element_type=F32)
        cov = jnp.where(same, gram / (n * length), 0.0)
        sums = jnp.concatenate(
            [jnp.sum(cov * eye, axis=0, keepdims=True), jnp.sum(cov * cov, axis=0, keepdims=True),
             jnp.zeros((6, LANES), F32)], axis=0,
        )
        sums = jnp.dot(sums, ones, precision=lax.Precision.HIGHEST, preferred_element_type=F32)
        trace, squares = sums[0:1], sums[1:2]
        ridge = RIDGE * trace / NB
        norm = jnp.sqrt(squares + 2.0 * ridge * trace + NB * ridge * ridge)
        norms.append(norm)
        estimate.append((cov + ridge * eye) / norm)
    for repeat in range(NS_ITERS):
        if repeat == 0:
            middle = [1.5 * eye - 0.5 * estimate[c] for c in packs]
        else:
            middle = [1.5 * eye - 0.5 * mul(inverse[c], estimate[c]) for c in packs]
        if repeat < NS_ITERS - 1:
            estimate = [mul(estimate[c], middle[c]) for c in packs]
        inverse = middle if repeat == 0 else [mul(middle[c], inverse[c]) for c in packs]

    base = len(packs) * 2 * blocks
    tile = LANES // NB
    fold = ((row_id % NB) == (lane_id % NB)).astype(F32).astype(BF16)
    spread = []
    whitenings = [inverse[c] / jnp.sqrt(norms[c]) for c in packs]
    for c in packs:
        wide = jnp.dot(whitenings[c].astype(BF16), fold, preferred_element_type=F32)
        spread.append(jnp.where(lane_id // NB == row_id % tile, wide, 0.0).astype(BF16))
    tiles = NB // tile
    held = len(packs) * PACK
    to = lax.broadcasted_iota(jnp.int32, (tiles * held, held * NB), 0)
    source = lax.broadcasted_iota(jnp.int32, (tiles * held, held * NB), 1)
    gather = (source // NB == to % held) & ((source % NB) // tile == to // held)
    flat = jnp.dot(
        gather.astype(F32).astype(BF16), jnp.concatenate(spread, axis=0), preferred_element_type=F32
    ).astype(BF16)
    for seg in range(n):
        out_ref[seg, base:base + tiles * held, :] = flat
    for c in packs:
        whitening = whitenings[c]
        right = jnp.concatenate(halves(whitening), axis=1)
        for i in range(blocks):
            y = stored[c, i * STEP * n:(i + 1) * STEP * n, :]
            rows_white = nt_dot(jnp.concatenate([y, y], axis=1), right)
            for b in range(STEP):
                w = rows_white[b * n:(b + 1) * n]
                white[c, b, i * n:(i + 1) * n, :] = w.astype(BF16)
                white[c, b, (blocks + i) * n:(blocks + i + 1) * n, :] = up(w).astype(BF16)

    reach = taps + STEP - 1
    fetch_weights.wait()
    size = blocks * n
    for c in packs:
        acc = jnp.zeros((size, STEP * rows), F32)
        for u in range(0, reach, 2):
            pair = [u] if u + 1 == reach else [u, u + 1]
            acc = acc + jnp.dot(
                jnp.concatenate(
                    [white[c, v % STEP, (v // STEP) * n:(v // STEP) * n + size, :] for v in pair], axis=1
                ),
                jnp.concatenate(
                    [
                        jnp.concatenate(
                            [weights_ref[c, w * LANES:(w + 1) * LANES, :] for w in (v, v + STEP // 2)], axis=1
                        )
                        for v in pair
                    ],
                    axis=0,
                ),
                preferred_element_type=F32,
            )
        total[0] = acc[:, :LANES]
        total[1] = acc[:, LANES:]
        for seg in range(n):
            both = [total[h, pl.ds(seg, blocks, stride=n), :] for h in range(2)]
            out_ref[seg, c * 2 * blocks:(c + 1) * 2 * blocks, :] = jnp.concatenate(both, axis=0).astype(BF16)


def final_kernel(groups, per, rows, got_ref, scores_ref, whitening_ref, joined, wide):
    n = got_ref.shape[0]
    packs = -(-groups // PACK)
    length, columns = scores_ref.shape
    blocks = length // STEP
    base = packs * 2 * blocks
    held = packs * PACK
    tiles = (NB * NB) // LANES
    for src in range(n):
        for k in range(tiles):
            at = base + k * held
            block = got_ref[src, base:base + tiles * held, :].astype(F32) if k == 0 else block
            joined[src * groups:(src + 1) * groups, k * LANES:(k + 1) * LANES] = (
                block[k * held:k * held + groups]
            )
    step = 2 * LANES
    row_id = lax.broadcasted_iota(jnp.int32, (step, step), 0)
    lane_id = lax.broadcasted_iota(jnp.int32, (step, step), 1)
    eye = (row_id == lane_id).astype(F32).astype(BF16)
    high = step // NB
    for k in range((NB * NB) // step):
        turned = nt_dot(eye, joined[:, k * step:(k + 1) * step].astype(BF16))
        whitening_ref[k * high:(k + 1) * high] = turned.reshape(high, NB, n * groups)
    each = min(PACK, groups) * per
    lane = lax.broadcasted_iota(jnp.int32, (blocks, LANES), 1)
    pieces = [(src, c) for src in range(n) for c in range(packs)]
    tiles = columns // LANES
    for h in range(2):
        loaded = {}
        for o in range(tiles):
            outs = [None] * (STEP // 2)
            for m in range((o * LANES) // each, min(len(pieces), -(-((o + 1) * LANES) // each))):
                if m not in loaded:
                    src, c = pieces[m]
                    loaded[m] = got_ref[src, c * 2 * blocks:(c + 1) * 2 * blocks, :].astype(F32)[
                        h * blocks:(h + 1) * blocks
                    ]
                at = m * each - o * LANES
                for q in range(STEP // 2):
                    shift = (at - q * rows) % LANES
                    moved = pltpu.roll(loaded[m], shift, 1) if shift else loaded[m]
                    if outs[q] is None:
                        outs[q] = moved
                    else:
                        outs[q] = jnp.where(lane >= at, moved, outs[q])
            for q in range(STEP // 2):
                tb = STEP - 1 - (h * (STEP // 2) + q)
                wide[o, pl.ds(tb, blocks, stride=STEP), :] = outs[q]
    for o in range(tiles):
        scores_ref[:, o * LANES:(o + 1) * LANES] = wide[o].astype(BF16)


def params(mib):
    return pltpu.CompilerParams(vmem_limit_bytes=mib * MIB)


def local(raw, pole, order, templates, support):
    length, channels = raw.shape
    n = lax.axis_size("tm")
    me = lax.axis_index("tm").astype(jnp.int32).reshape(1)
    all_groups = channels // NB
    groups = all_groups // n
    per = templates.shape[0] // all_groups
    taps = templates.shape[1]
    count = groups * per
    packs = -(-groups // PACK)
    rows = NB
    width = packs * LANES
    blocks = length // STEP

    if groups % PACK == 0:
        send = raw.reshape(length, n, width).transpose(1, 0, 2)
    else:
        pieces = [raw[:, (d * groups // 2) * 2 * NB:][:, :width] for d in range(n)]
        send = jnp.stack(pieces, axis=0)
    received = lax.all_to_all(send, "tm", 0, 0, tiled=True)

    vmem = pl.BlockSpec(memory_space=pltpu.VMEM)
    anywhere = pl.BlockSpec(memory_space=pl.ANY)
    tap_rows = (taps + 2 * STEP - 2 - (LANES // rows - 1)) * LANES
    by_lane = templates.transpose(1, 2, 0)
    used = support.T
    ends = by_lane.shape[2] // LANES - 1

    def left(s):
        return (s[0] * count) // LANES

    def right(s):
        return jnp.minimum((s[0] * count) // LANES + 1, ends)

    def whole(shape):
        return pl.BlockSpec(shape, lambda i, s: (0,) * len(shape))

    poles = pole.reshape(-1, LANES)
    weights = pl.pallas_call(
        functools.partial(template_kernel, groups, per, rows),
        out_shape=jax.ShapeDtypeStruct((packs, tap_rows, LANES), BF16),
        grid_spec=pltpu.PrefetchScalarGridSpec(
            num_scalar_prefetch=1,
            grid=(1,),
            in_specs=[
                pl.BlockSpec((taps, NB, LANES), lambda i, s: (0, 0, left(s))),
                pl.BlockSpec((taps, NB, LANES), lambda i, s: (0, 0, right(s))),
                pl.BlockSpec((NB, LANES), lambda i, s: (0, left(s))),
                pl.BlockSpec((NB, LANES), lambda i, s: (0, right(s))),
            ],
            out_specs=whole((packs, tap_rows, LANES)),
            scratch_shapes=[pltpu.VMEM(((taps + 2 * STEP - 2) * NB, width), BF16)],
        ),
        compiler_params=params(58),
        name="templates",
    )(me, by_lane, by_lane, used, used)
    picks, permuted = pl.pallas_call(
        functools.partial(order_kernel, groups),
        out_shape=[
            jax.ShapeDtypeStruct((packs, LANES, LANES), BF16),
            jax.ShapeDtypeStruct((packs, 8, LANES), F32),
        ],
        in_specs=[pl.BlockSpec(memory_space=pltpu.SMEM), vmem, vmem],
        out_specs=[vmem, vmem],
        compiler_params=params(16),
        name="order",
    )(me, order.T, poles)

    total_rows = n * length
    payload = jax.ShapeDtypeStruct((n, packs * (2 * blocks + NB), LANES), BF16)
    sent = pl.pallas_call(
        functools.partial(main_kernel, groups, rows, taps),
        out_shape=payload,
        in_specs=[anywhere, vmem, vmem, anywhere],
        out_specs=vmem,
        scratch_shapes=[
            pltpu.VMEM((n, length, width), BF16),
            pltpu.VMEM((packs, tap_rows, LANES), BF16),
            pltpu.VMEM((packs, total_rows, LANES), F32),
            pltpu.VMEM((packs, total_rows, LANES), F32),
            pltpu.VMEM((packs, total_rows, LANES), BF16),
            pltpu.VMEM((packs, STEP, 2 * blocks * n, LANES), BF16),
            pltpu.VMEM((2, blocks * n, LANES), F32),
            pltpu.SemaphoreType.DMA((2,)),
        ],
        compiler_params=params(52),
        name="filter_whiten_match",
    )(received, picks, permuted, weights)
    got = lax.all_to_all(sent, "tm", 0, 0, tiled=True)

    columns = all_groups * per
    scores, whitening = pl.pallas_call(
        functools.partial(final_kernel, groups, per, rows),
        out_shape=[
            jax.ShapeDtypeStruct((length, columns), BF16),
            jax.ShapeDtypeStruct((NB, NB, all_groups), F32),
        ],
        in_specs=[vmem],
        out_specs=[vmem, vmem],
        scratch_shapes=[
            pltpu.VMEM((all_groups, NB * NB), F32),
            pltpu.VMEM((columns // LANES, length, LANES), F32),
        ],
        compiler_params=params(28),
        name="unpack",
    )(got)
    return scores, whitening.transpose(2, 0, 1)


def solution(mesh):
    in_specs = (P(("rec", "tm"), None), P(), P(), P(), P())
    out_specs = (P(("rec", "tm"), None), P("rec", None, None))
    return jax.shard_map(local, mesh=mesh, in_specs=in_specs, out_specs=out_specs, check_vma=False)
```

```python
import functools

import jax
import jax.numpy as jnp
from jax import lax
from jax.experimental import pallas as pl
from jax.experimental.pallas import tpu as pltpu
from jax.sharding import PartitionSpec as P

NB = 32
PACK = 4
LANES = NB * PACK
STEP = 8
NS_ITERS = 4
RIDGE = 0.1
MIB = 1024 * 1024
F32, BF16 = jnp.float32, jnp.bfloat16


def nt_dot(a, b):
    return lax.dot_general(a, b, (((1,), (1,)), ((), ())), preferred_element_type=F32)


def halves(a):
    high = a.astype(BF16)
    return high, (a - high.astype(F32)).astype(BF16)


def mul(a, b):
    a_high, a_low = halves(a)
    b_high, b_low = halves(b)
    right = jnp.concatenate([b_high, b_low], axis=1)
    out = jnp.dot(
        jnp.concatenate([a_high, a_low], axis=1),
        jnp.concatenate([right, right], axis=0),
        preferred_element_type=F32,
    )
    return out[:, :LANES] + out[:, LANES:]


def down(v, distance):
    zeros = jnp.zeros((distance, v.shape[1]), v.dtype)
    return jnp.concatenate([zeros, v[:-distance]], axis=0)


def up(v):
    return jnp.concatenate([v[1:], jnp.zeros((1, v.shape[1]), v.dtype)], axis=0)


def layout(groups, width, blocks):
    score_tiles = width // LANES
    diagonal_at = score_tiles * blocks
    return score_tiles, diagonal_at, -(-(diagonal_at + blocks) // 16) * 16


def template_kernel(
    groups, per, rows, mine, left_ref, right_ref, left_used, right_used, weights_ref, lined
):
    taps = left_ref.shape[0]
    packs = weights_ref.shape[0]
    me = mine[0]
    count = groups * per
    lane = lax.broadcasted_iota(jnp.int32, (2 * LANES, packs * LANES), 1)
    row = lax.broadcasted_iota(jnp.int32, (2 * LANES, packs * LANES), 0)
    number = (lane // LANES) * PACK * per + lane % rows
    real = (lane % rows < PACK * per) & (number < count)
    base = ((me * count) // LANES) * LANES
    select = (real & (base + row == me * count + number)).astype(F32).astype(BF16)
    used = jnp.concatenate([left_used[...], right_used[...]], axis=1).astype(F32).astype(BF16)
    pad = (STEP - 1) * NB
    lined[:pad, :] = jnp.zeros((pad, packs * LANES), BF16)
    lined[pad + taps * NB:, :] = jnp.zeros((pad, packs * LANES), BF16)
    for s in range(0, taps, STEP):
        group = range(s, min(taps, s + STEP))
        blocks = [jnp.concatenate([left_ref[t], right_ref[t]], axis=1) * used for t in group]
        picked = jnp.dot(jnp.concatenate(blocks, axis=0), select, preferred_element_type=F32)
        lined[pad + s * NB:pad + (s + len(group)) * NB, :] = picked.astype(BF16)
    lane = lax.broadcasted_iota(jnp.int32, (NB, LANES), 1)
    taken = [(lane // rows == k).astype(F32).astype(BF16) for k in range(LANES // rows)]
    owned = [((lane % rows) // per == g).astype(F32).astype(BF16) for g in range(PACK)]
    for v in range(weights_ref.shape[1] // LANES):
        for c in range(packs):
            block = sum(
                lined[(v + k) * NB:(v + k + 1) * NB, c * LANES:(c + 1) * LANES] * taken[k]
                for k in range(LANES // rows)
            )
            for g in range(PACK):
                weights_ref[c, v * LANES + g * NB:v * LANES + (g + 1) * NB, :] = block * owned[g]


def order_kernel(groups, per, rows, mine, order_ref, pole_ref, picks_ref, poles_ref, places_ref, turns_ref):
    row = lax.broadcasted_iota(jnp.int32, (places_ref.shape[0], 1), 0)
    number = (row // (STEP * rows)) * PACK * per + row % rows
    held = (row % rows < PACK * per) & (number < groups * per)
    place = jnp.where(held, ((row % (STEP * rows)) // rows) * groups * per + number, -1)
    lane = lax.broadcasted_iota(jnp.int32, places_ref.shape, 1)
    places_ref[...] = (lane == place).astype(F32).astype(BF16)
    row = lax.broadcasted_iota(jnp.int32, (NB * NB, 1), 0)
    low = jnp.minimum(row // NB, row % NB)
    high = jnp.maximum(row // NB, row % NB)
    half = NB // 2
    place = jnp.where(low < high, (high - half) * NB + low - half, half * NB + low)
    place = jnp.where(low < half, low * NB + high, place)
    lane = lax.broadcasted_iota(jnp.int32, turns_ref.shape, 1)
    turns_ref[...] = (lane == place).astype(F32).astype(BF16)
    me = mine[0]
    packs = picks_ref.shape[0]
    length, blocks = order_ref.shape
    lane = lax.broadcasted_iota(jnp.int32, (length, blocks), 1)
    ids_lane = lax.broadcasted_iota(jnp.int32, (LANES, LANES), 1)
    for c in range(packs):
        start = me * groups + PACK * c
        block = start // 2
        ids = jnp.concatenate(
            [
                jnp.sum(jnp.where(lane == block + k, order_ref[...], 0), axis=1, keepdims=True) + length * k
                for k in range(2)
            ],
            axis=0,
        )
        pole = pole_ref[pl.ds(block // 2, 1), :]
        if groups % PACK:
            last = pole_ref.shape[0] - 1
            after = pole_ref[pl.ds(jnp.minimum(block // 2 + 1, last), 1), :]
            joined = jnp.concatenate([pole[:, length:], after[:, :length]], axis=1)
            pole = jnp.where(block % 2 == 1, joined, pole)
            ids = jnp.where(start % 2 == 1, jnp.concatenate([ids[NB:], ids[:NB]], axis=0), ids)
        pick = (ids_lane == ids).astype(F32)
        picks_ref[c] = pick.astype(BF16)
        poles_ref[c] = lax.dot_general(
            jnp.broadcast_to(pole, (8, LANES)), pick, (((1,), (1,)), ((), ())),
            precision=lax.Precision.HIGHEST, preferred_element_type=F32,
        )


def main_kernel(
    groups, rows, taps, raw_any, picks_ref, poles_ref, places_any, weights_any, out_ref,
    raw_ref, places_ref, weights_ref, first, state, stored, white, total, sems,
):
    n, length, width = raw_ref.shape
    fetch_raw = pltpu.make_async_copy(raw_any, raw_ref, sems.at[0])
    fetch_weights = pltpu.make_async_copy(weights_any, weights_ref, sems.at[1])
    fetch_places = pltpu.make_async_copy(places_any, places_ref, sems.at[2])
    fetch_raw.start()
    packs = range(width // LANES)
    blocks = length // STEP
    row_id = lax.broadcasted_iota(jnp.int32, (LANES, LANES), 0)
    lane_id = lax.broadcasted_iota(jnp.int32, (LANES, LANES), 1)
    same = (row_id // NB) == (lane_id // NB)
    eye = (row_id == lane_id).astype(F32)
    ones = same.astype(F32)
    poles = [jnp.broadcast_to(poles_ref[c, :1, :], (n, LANES)) for c in packs]
    gains = [0.5 * (1.0 + pole) for pole in poles]
    fetch_raw.wait()
    fetch_weights.start()
    fetch_places.start()
    for c in packs:
        part = raw_ref[:, :, c * LANES:(c + 1) * LANES].reshape(n * length, LANES)
        first[c] = nt_dot(part, picks_ref[c])

    level = [jnp.zeros((n, LANES), F32) for c in packs]
    last = [down(first[c, pl.ds(length - 1, n, stride=length), :], 1) for c in packs]
    for j in range(length):
        for c in packs:
            now = first[c, pl.ds(j, n, stride=length), :]
            level[c] = poles[c] * level[c] + gains[c] * (now - last[c])
            last[c] = now
            state[c, j * n:(j + 1) * n, :] = level[c]
    incoming = []
    for c in packs:
        span, square, left = None, poles[c], length
        while left:
            if left % 2:
                span = square if span is None else span * square
            square = square * square
            left //= 2
        value, distance = level[c], 1
        while distance < n:
            value = value + span * down(value, distance)
            span = span * span
            distance *= 2
        incoming.append(down(value, 1))
    carried = list(incoming)
    for j in range(length):
        for c in packs:
            carried[c] = carried[c] * poles[c]
            stored[c, j * n:(j + 1) * n, :] = (state[c, j * n:(j + 1) * n, :] + carried[c]).astype(BF16)

    estimate, inverse, norms = [], [], []
    for c in packs:
        y = stored[c]
        gram = lax.dot_general(y, y, (((0,), (0,)), ((), ())), preferred_element_type=F32)
        cov = jnp.where(same, gram / (n * length), 0.0)
        sums = jnp.concatenate(
            [jnp.sum(cov * eye, axis=0, keepdims=True), jnp.sum(cov * cov, axis=0, keepdims=True),
             jnp.zeros((6, LANES), F32)], axis=0,
        )
        sums = jnp.dot(sums, ones, precision=lax.Precision.HIGHEST, preferred_element_type=F32)
        trace, squares = sums[0:1], sums[1:2]
        ridge = RIDGE * trace / NB
        norm = jnp.sqrt(squares + 2.0 * ridge * trace + NB * ridge * ridge)
        norms.append(norm)
        estimate.append((cov + ridge * eye) / norm)
    for repeat in range(NS_ITERS):
        if repeat == 0:
            middle = [1.5 * eye - 0.5 * estimate[c] for c in packs]
        else:
            middle = [1.5 * eye - 0.5 * mul(inverse[c], estimate[c]) for c in packs]
        if repeat < NS_ITERS - 1:
            estimate = [mul(estimate[c], middle[c]) for c in packs]
        inverse = middle if repeat == 0 else [mul(middle[c], inverse[c]) for c in packs]

    score_tiles, diagonal_at, flat_at = layout(groups, places_ref.shape[1], blocks)
    tile, half = LANES // NB, NB // 2
    folded = row_id % NB
    fold = jnp.concatenate([folded == lane_id % NB, folded == lane_id % NB + half], axis=1).astype(F32).astype(BF16)
    j, k = row_id % NB, lane_id % NB
    quarter = lane_id // NB
    spread, diagonals = [], []
    whitenings = [inverse[c] / jnp.sqrt(norms[c]) for c in packs]
    for c in packs:
        wide = jnp.dot(whitenings[c].astype(BF16), fold, preferred_element_type=F32)
        upper = jnp.where((j < half) & (k >= j), wide[:, :LANES], 0.0)
        lower = jnp.where(k < j - half, wide[:, LANES:], 0.0)
        spread.append(jnp.where(quarter == row_id % tile, upper + lower, 0.0).astype(BF16))
        group = c * PACK + row_id // NB
        diagonals.append(
            jnp.where((quarter == group // 8) & (j == k), wide[:, :LANES], 0.0).astype(BF16)
        )
    tiles = half // tile
    held = len(packs) * PACK
    to = lax.broadcasted_iota(jnp.int32, (tiles * held, held * NB), 0)
    source = lax.broadcasted_iota(jnp.int32, (tiles * held, held * NB), 1)
    gather = (source // NB == to % held) & ((source % half) // tile == to // held)
    flat = jnp.dot(
        gather.astype(F32).astype(BF16), jnp.concatenate(spread, axis=0), preferred_element_type=F32
    ).astype(BF16)
    for seg in range(n):
        out_ref[seg, flat_at:flat_at + tiles * held, :] = flat
    to = lax.broadcasted_iota(jnp.int32, (8, held * NB), 0)
    source = lax.broadcasted_iota(jnp.int32, (8, held * NB), 1)
    diagonal = jnp.dot(
        ((source // NB) % 8 == to).astype(F32).astype(BF16), jnp.concatenate(diagonals, axis=0),
        preferred_element_type=F32,
    )
    for c in packs:
        whitening = whitenings[c]
        right = jnp.concatenate(halves(whitening), axis=1)
        for i in range(blocks):
            y = stored[c, i * STEP * n:(i + 1) * STEP * n, :]
            rows_white = nt_dot(jnp.concatenate([y, y], axis=1), right)
            for b in range(STEP):
                w = rows_white[b * n:(b + 1) * n]
                white[c, b, i * n:(i + 1) * n, :] = w.astype(BF16)
                white[c, b, (blocks + i) * n:(blocks + i + 1) * n, :] = up(w).astype(BF16)

    reach = taps + STEP - 1
    fetch_weights.wait()
    fetch_places.wait()
    size = blocks * n
    for c in packs:
        acc = jnp.zeros((size, STEP * rows), F32)
        for u in range(0, reach, 2):
            pair = [u] if u + 1 == reach else [u, u + 1]
            acc = acc + jnp.dot(
                jnp.concatenate(
                    [white[c, v % STEP, (v // STEP) * n:(v // STEP) * n + size, :] for v in pair], axis=1
                ),
                jnp.concatenate(
                    [
                        jnp.concatenate(
                            [weights_ref[c, w * LANES:(w + 1) * LANES, :] for w in (v, v + STEP // 2)], axis=1
                        )
                        for v in pair
                    ],
                    axis=0,
                ),
                preferred_element_type=F32,
            )
        placed = jnp.dot(
            acc.astype(BF16), places_ref[c * STEP * rows:(c + 1) * STEP * rows, :], preferred_element_type=F32
        )
        packed = placed if c == 0 else packed + placed
    for t in range(score_tiles):
        total[t] = packed[:, t * LANES:(t + 1) * LANES]
    for seg in range(n):
        parts = [total[t, pl.ds(seg, blocks, stride=n), :] for t in range(score_tiles)] + [diagonal]
        if len(parts) % 2:
            parts.append(jnp.zeros_like(diagonal))
        for t in range(0, len(parts), 2):
            both = jnp.concatenate(parts[t:t + 2], axis=0).astype(BF16)
            out_ref[seg, t * blocks:(t + 2) * blocks, :] = both


def final_kernel(groups, per, width, got_ref, turns_ref, scores_ref, whitening_ref, joined, wide):
    n = got_ref.shape[0]
    held = -(-groups // PACK) * PACK
    length, columns = scores_ref.shape
    blocks = length // STEP
    score_tiles, diagonal_at, flat_at = layout(groups, width, blocks)
    tiles = NB // 2 * NB // LANES
    aligned = diagonal_at // 16 * 16
    joined[:, tiles * LANES:] = jnp.zeros((n * groups, LANES), F32)
    for src in range(n):
        flat = got_ref[src, flat_at:flat_at + tiles * held, :].astype(F32)
        for k in range(tiles):
            joined[src * groups:(src + 1) * groups, k * LANES:(k + 1) * LANES] = (
                flat[k * held:k * held + groups]
            )
        ends = got_ref[src, aligned:aligned + 16, :].astype(F32)[diagonal_at - aligned:]
        for q in range(-(-groups // 8)):
            some = min(8, groups - 8 * q)
            joined[src * groups + 8 * q:src * groups + 8 * q + some, tiles * LANES:tiles * LANES + NB] = (
                ends[:some, q * NB:(q + 1) * NB]
            )
    entries = joined[...].astype(BF16)
    step = 2 * LANES
    high = step // NB
    for k in range((NB * NB) // step):
        turned = nt_dot(turns_ref[k * step:(k + 1) * step, :], entries)
        whitening_ref[k * high:(k + 1) * high] = turned.reshape(high, NB, n * groups)

    each = groups * per
    lane = lax.broadcasted_iota(jnp.int32, (blocks, LANES), 1)
    for o in range(columns // LANES):
        for tb in range(STEP):
            out = None
            at = o * LANES
            while at < (o + 1) * LANES:
                src = at // each
                begin = tb * each + at - src * each
                t = begin // LANES
                stop = min((o + 1) * LANES, (src + 1) * each, at + (t + 1) * LANES - begin)
                some = got_ref[src, t // 2 * 16:t // 2 * 16 + 16, :].astype(F32)[t % 2 * 8:t % 2 * 8 + 8]
                shift = (at - begin) % LANES
                moved = pltpu.roll(some, shift, 1) if shift else some
                out = moved if out is None else jnp.where(lane >= at - o * LANES, moved, out)
                at = stop
            wide[o, pl.ds(STEP - 1 - tb, blocks, stride=STEP), :] = out
    for o in range(columns // LANES):
        scores_ref[:, o * LANES:(o + 1) * LANES] = wide[o].astype(BF16)


def params(mib):
    return pltpu.CompilerParams(vmem_limit_bytes=mib * MIB)


def local(raw, pole, order, templates, support):
    length, channels = raw.shape
    n = lax.axis_size("tm")
    me = lax.axis_index("tm").astype(jnp.int32).reshape(1)
    all_groups = channels // NB
    groups = all_groups // n
    per = templates.shape[0] // all_groups
    taps = templates.shape[1]
    count = groups * per
    packs = -(-groups // PACK)
    rows = NB
    width = packs * LANES
    blocks = length // STEP

    if groups % PACK == 0:
        send = raw.reshape(length, n, width).transpose(1, 0, 2)
    else:
        pieces = [raw[:, (d * groups // 2) * 2 * NB:][:, :width] for d in range(n)]
        send = jnp.stack(pieces, axis=0)
    received = lax.all_to_all(send, "tm", 0, 0, tiled=True)

    vmem = pl.BlockSpec(memory_space=pltpu.VMEM)
    anywhere = pl.BlockSpec(memory_space=pl.ANY)
    tap_rows = (taps + 2 * STEP - 2 - (LANES // rows - 1)) * LANES
    by_lane = templates.transpose(1, 2, 0)
    used = support.T
    ends = by_lane.shape[2] // LANES - 1

    def left(s):
        return (s[0] * count) // LANES

    def right(s):
        return jnp.minimum((s[0] * count) // LANES + 1, ends)

    def whole(shape):
        return pl.BlockSpec(shape, lambda i, s: (0,) * len(shape))

    poles = pole.reshape(-1, LANES)
    weights = pl.pallas_call(
        functools.partial(template_kernel, groups, per, rows),
        out_shape=jax.ShapeDtypeStruct((packs, tap_rows, LANES), BF16),
        grid_spec=pltpu.PrefetchScalarGridSpec(
            num_scalar_prefetch=1,
            grid=(1,),
            in_specs=[
                pl.BlockSpec((taps, NB, LANES), lambda i, s: (0, 0, left(s))),
                pl.BlockSpec((taps, NB, LANES), lambda i, s: (0, 0, right(s))),
                pl.BlockSpec((NB, LANES), lambda i, s: (0, left(s))),
                pl.BlockSpec((NB, LANES), lambda i, s: (0, right(s))),
            ],
            out_specs=whole((packs, tap_rows, LANES)),
            scratch_shapes=[pltpu.VMEM(((taps + 2 * STEP - 2) * NB, width), BF16)],
        ),
        compiler_params=params(58),
        name="templates",
    )(me, by_lane, by_lane, used, used)
    score_width = -(-STEP * count // LANES) * LANES
    _, _, flat_at = layout(groups, score_width, blocks)
    sent_rows = -(-(flat_at + packs * PACK * NB // 2 * NB // LANES) // 16) * 16
    picks, permuted, places, turns = pl.pallas_call(
        functools.partial(order_kernel, groups, per, rows),
        out_shape=[
            jax.ShapeDtypeStruct((packs, LANES, LANES), BF16),
            jax.ShapeDtypeStruct((packs, 8, LANES), F32),
            jax.ShapeDtypeStruct((packs * STEP * rows, score_width), BF16),
            jax.ShapeDtypeStruct((NB * NB, NB // 2 * NB + LANES), BF16),
        ],
        in_specs=[pl.BlockSpec(memory_space=pltpu.SMEM), vmem, vmem],
        out_specs=[vmem] * 4,
        compiler_params=params(16),
        name="order",
    )(me, order.T, poles)

    total_rows = n * length
    payload = jax.ShapeDtypeStruct((n, sent_rows, LANES), BF16)
    sent = pl.pallas_call(
        functools.partial(main_kernel, groups, rows, taps),
        out_shape=payload,
        in_specs=[anywhere, vmem, vmem, anywhere, anywhere],
        out_specs=vmem,
        scratch_shapes=[
            pltpu.VMEM((n, length, width), BF16),
            pltpu.VMEM((packs * STEP * rows, score_width), BF16),
            pltpu.VMEM((packs, tap_rows, LANES), BF16),
            pltpu.VMEM((packs, total_rows, LANES), F32),
            pltpu.VMEM((packs, total_rows, LANES), F32),
            pltpu.VMEM((packs, total_rows, LANES), BF16),
            pltpu.VMEM((packs, STEP, 2 * blocks * n, LANES), BF16),
            pltpu.VMEM((score_width // LANES, blocks * n, LANES), F32),
            pltpu.SemaphoreType.DMA((3,)),
        ],
        compiler_params=params(52),
        name="filter_whiten_match",
    )(received, picks, permuted, places, weights)
    got = lax.all_to_all(sent, "tm", 0, 0, tiled=True)

    columns = all_groups * per
    scores, whitening = pl.pallas_call(
        functools.partial(final_kernel, groups, per, score_width),
        out_shape=[
            jax.ShapeDtypeStruct((length, columns), BF16),
            jax.ShapeDtypeStruct((NB, NB, all_groups), F32),
        ],
        in_specs=[vmem, vmem],
        out_specs=[vmem, vmem],
        scratch_shapes=[
            pltpu.VMEM((all_groups, NB // 2 * NB + LANES), F32),
            pltpu.VMEM((columns // LANES, length, LANES), F32),
        ],
        compiler_params=params(28),
        name="unpack",
    )(got, turns)
    return scores, whitening.transpose(2, 0, 1)


def solution(mesh):
    in_specs = (P(("rec", "tm"), None), P(), P(), P(), P())
    out_specs = (P(("rec", "tm"), None), P("rec", None, None))
    return jax.shard_map(local, mesh=mesh, in_specs=in_specs, out_specs=out_specs, check_vma=False)
```

```python
import functools

import jax
import jax.numpy as jnp
from jax import lax
from jax.experimental import pallas as pl
from jax.experimental.pallas import tpu as pltpu
from jax.sharding import PartitionSpec as P

NB = 32
PACK = 4
LANES = NB * PACK
STEP = 8
NS_ITERS = 4
RIDGE = 0.1
MIB = 1024 * 1024
F32, BF16 = jnp.float32, jnp.bfloat16


def nt_dot(a, b):
    return lax.dot_general(a, b, (((1,), (1,)), ((), ())), preferred_element_type=F32)


def halves(a):
    high = a.astype(BF16)
    return high, (a - high.astype(F32)).astype(BF16)


def mul(several, b):
    b_high, b_low = halves(b)
    right = jnp.concatenate([b_high, b_low], axis=1)
    left = [jnp.concatenate(halves(a), axis=1) for a in several]
    out = jnp.dot(
        jnp.concatenate(left, axis=0), jnp.concatenate([right, right], axis=0), preferred_element_type=F32
    )
    out = out[:, :LANES] + out[:, LANES:]
    return [out[k * LANES:(k + 1) * LANES] for k in range(len(several))]


def down(v, distance):
    zeros = jnp.zeros((distance, v.shape[1]), v.dtype)
    return jnp.concatenate([zeros, v[:-distance]], axis=0)


def up(v):
    return jnp.concatenate([v[1:], jnp.zeros((1, v.shape[1]), v.dtype)], axis=0)


def layout(groups, width, blocks):
    score_tiles = width // LANES
    half_rows = (NB // 2 * NB // LANES // 2) * (-(-groups // PACK) * PACK)
    return score_tiles * blocks, half_rows, -(-(score_tiles * blocks + half_rows) // 16) * 16


def template_kernel(
    groups, per, rows, mine, left_ref, right_ref, left_used, right_used, weights_ref, lined
):
    taps = left_ref.shape[0]
    packs = weights_ref.shape[0]
    me = mine[0]
    count = groups * per
    lane = lax.broadcasted_iota(jnp.int32, (2 * LANES, packs * LANES), 1)
    row = lax.broadcasted_iota(jnp.int32, (2 * LANES, packs * LANES), 0)
    number = (lane // LANES) * PACK * per + lane % rows
    real = (lane % rows < PACK * per) & (number < count)
    base = ((me * count) // LANES) * LANES
    select = (real & (base + row == me * count + number)).astype(F32).astype(BF16)
    used = jnp.concatenate([left_used[...], right_used[...]], axis=1).astype(F32).astype(BF16)
    pad = (STEP - 1) * NB
    lined[:pad, :] = jnp.zeros((pad, packs * LANES), BF16)
    lined[pad + taps * NB:, :] = jnp.zeros((pad, packs * LANES), BF16)
    for s in range(0, taps, STEP):
        group = range(s, min(taps, s + STEP))
        blocks = [jnp.concatenate([left_ref[t], right_ref[t]], axis=1) * used for t in group]
        picked = jnp.dot(jnp.concatenate(blocks, axis=0), select, preferred_element_type=F32)
        lined[pad + s * NB:pad + (s + len(group)) * NB, :] = picked.astype(BF16)
    lane = lax.broadcasted_iota(jnp.int32, (NB, LANES), 1)
    taken = [(lane // rows == k).astype(F32).astype(BF16) for k in range(LANES // rows)]
    owned = [((lane % rows) // per == g).astype(F32).astype(BF16) for g in range(PACK)]
    for v in range(weights_ref.shape[1] // LANES):
        for c in range(packs):
            block = sum(
                lined[(v + k) * NB:(v + k + 1) * NB, c * LANES:(c + 1) * LANES] * taken[k]
                for k in range(LANES // rows)
            )
            for g in range(PACK):
                weights_ref[c, v * LANES + g * NB:v * LANES + (g + 1) * NB, :] = block * owned[g]


def order_kernel(groups, per, rows, mine, order_ref, pole_ref, picks_ref, poles_ref, places_ref, turns_ref):
    me = mine[0]
    row = lax.broadcasted_iota(jnp.int32, (places_ref.shape[0], 1), 0)
    number = (row // (STEP * rows)) * PACK * per + row % rows
    held = (row % rows < PACK * per) & (number < groups * per)
    place = jnp.where(held, ((row % (STEP * rows)) // rows) * groups * per + number, -1)
    lane = lax.broadcasted_iota(jnp.int32, places_ref.shape, 1)
    places_ref[...] = (lane == place).astype(F32).astype(BF16)
    row = lax.broadcasted_iota(jnp.int32, (NB * NB, 1), 0)
    low = jnp.minimum(row // NB, row % NB)
    high = jnp.maximum(row // NB, row % NB)
    half = NB // 2
    place = jnp.where(low < high, (high - half) * NB + low - half, half * NB + low)
    place = jnp.where(low < half, low * NB + high, place)
    quarter = half * NB // 2
    swapped = jnp.where(place < quarter, place + quarter, place - quarter)
    place = jnp.where((me % 2 == 1) & (place < half * NB), swapped, place)
    lane = lax.broadcasted_iota(jnp.int32, turns_ref.shape, 1)
    turns_ref[...] = (lane == place).astype(F32).astype(BF16)
    packs = picks_ref.shape[0]
    length, blocks = order_ref.shape
    lane = lax.broadcasted_iota(jnp.int32, (length, blocks), 1)
    ids_lane = lax.broadcasted_iota(jnp.int32, (LANES, LANES), 1)
    for c in range(packs):
        start = me * groups + PACK * c
        block = start // 2
        ids = jnp.concatenate(
            [
                jnp.sum(jnp.where(lane == block + k, order_ref[...], 0), axis=1, keepdims=True) + length * k
                for k in range(2)
            ],
            axis=0,
        )
        pole = pole_ref[pl.ds(block // 2, 1), :]
        if groups % PACK:
            last = pole_ref.shape[0] - 1
            after = pole_ref[pl.ds(jnp.minimum(block // 2 + 1, last), 1), :]
            joined = jnp.concatenate([pole[:, length:], after[:, :length]], axis=1)
            pole = jnp.where(block % 2 == 1, joined, pole)
            ids = jnp.where(start % 2 == 1, jnp.concatenate([ids[NB:], ids[:NB]], axis=0), ids)
        pick = (ids_lane == ids).astype(F32)
        picks_ref[c] = pick.astype(BF16)
        poles_ref[c] = lax.dot_general(
            jnp.broadcast_to(pole, (8, LANES)), pick, (((1,), (1,)), ((), ())),
            precision=lax.Precision.HIGHEST, preferred_element_type=F32,
        )


def main_kernel(
    groups, rows, taps, raw_ref, picks_ref, poles_ref, places_any, weights_any, out_ref,
    places_ref, weights_ref, first, state, stored, white, total, sems,
):
    n, length, width = raw_ref.shape
    fetch_weights = pltpu.make_async_copy(weights_any, weights_ref, sems.at[0])
    fetch_places = pltpu.make_async_copy(places_any, places_ref, sems.at[1])
    packs = range(width // LANES)
    blocks = length // STEP
    row_id = lax.broadcasted_iota(jnp.int32, (LANES, LANES), 0)
    lane_id = lax.broadcasted_iota(jnp.int32, (LANES, LANES), 1)
    same = (row_id // NB) == (lane_id // NB)
    eye = (row_id == lane_id).astype(F32)
    ones = same.astype(F32).astype(BF16)
    poles = [jnp.broadcast_to(poles_ref[c, :1, :], (n, LANES)) for c in packs]
    gains = [0.5 * (1.0 + pole) for pole in poles]
    fetch_weights.start()
    fetch_places.start()
    for c in packs:
        part = raw_ref[:, :, c * LANES:(c + 1) * LANES].reshape(n * length, LANES)
        first[c] = nt_dot(part, picks_ref[c])

    level = [jnp.zeros((n, LANES), F32) for c in packs]
    last = [down(first[c, pl.ds(length - 1, n, stride=length), :], 1) for c in packs]
    for j in range(length):
        for c in packs:
            now = first[c, pl.ds(j, n, stride=length), :]
            level[c] = poles[c] * level[c] + gains[c] * (now - last[c])
            last[c] = now
            state[c, j * n:(j + 1) * n, :] = level[c]
    incoming = []
    for c in packs:
        span, square, left = None, poles[c], length
        while left:
            if left % 2:
                span = square if span is None else span * square
            square = square * square
            left //= 2
        value, distance = level[c], 1
        while distance < n:
            value = value + span * down(value, distance)
            span = span * span
            distance *= 2
        incoming.append(down(value, 1))
    carried = list(incoming)
    for j in range(length):
        for c in packs:
            carried[c] = carried[c] * poles[c]
            stored[c, j * n:(j + 1) * n, :] = (state[c, j * n:(j + 1) * n, :] + carried[c]).astype(BF16)

    estimate, inverse, norms = [], [], []
    for c in packs:
        y = stored[c]
        gram = lax.dot_general(y, y, (((0,), (0,)), ((), ())), preferred_element_type=F32)
        cov = jnp.where(same, gram * (1.0 / (n * length)), 0.0)
        sums = jnp.concatenate(
            [jnp.sum(cov * eye, axis=0, keepdims=True), jnp.sum(cov * cov, axis=0, keepdims=True),
             jnp.zeros((6, LANES), F32)], axis=0,
        )
        sums = jnp.dot(jnp.concatenate(halves(sums), axis=0), ones, preferred_element_type=F32)
        sums = sums[:8] + sums[8:]
        trace, squares = sums[0:1], sums[1:2]
        ridge = RIDGE * trace / NB
        norm = jnp.sqrt(squares + 2.0 * ridge * trace + NB * ridge * ridge)
        norms.append(norm)
        estimate.append((cov + ridge * eye) * (1.0 / norm))
    for repeat in range(NS_ITERS):
        if repeat == 0:
            inverse = [1.5 * eye - 0.5 * estimate[c] for c in packs]
            estimate = [mul([estimate[c]], inverse[c])[0] for c in packs]
            continue
        middle = [1.5 * eye - 0.5 * mul([inverse[c]], estimate[c])[0] for c in packs]
        if repeat < NS_ITERS - 1:
            both = [mul([inverse[c], estimate[c]], middle[c]) for c in packs]
            inverse, estimate = [pair[0] for pair in both], [pair[1] for pair in both]
        else:
            inverse = [mul([inverse[c]], middle[c])[0] for c in packs]

    score_tiles = places_ref.shape[1] // LANES
    score_rows, half_rows, sent_rows = layout(groups, places_ref.shape[1], blocks)
    tile, half = LANES // NB, NB // 2
    folded = row_id % NB
    fold = jnp.concatenate([folded == lane_id % NB, folded == lane_id % NB + half], axis=1).astype(F32).astype(BF16)
    j, k = row_id % NB, lane_id % NB
    quarter = lane_id // NB
    spread, diagonals = [], []
    whitenings = [inverse[c] * (1.0 / jnp.sqrt(norms[c])) for c in packs]
    for c in packs:
        wide = jnp.dot(whitenings[c].astype(BF16), fold, preferred_element_type=F32)
        upper = jnp.where((j < half) & (k >= j), wide[:, :LANES], 0.0)
        lower = jnp.where(k < j - half, wide[:, LANES:], 0.0)
        spread.append(jnp.where(quarter == row_id % tile, upper + lower, 0.0).astype(BF16))
        group = c * PACK + row_id // NB
        diagonals.append(
            jnp.where((quarter == tile // 2 + group // 8) & (j == k), wide[:, :LANES], 0.0).astype(BF16)
        )
    tiles = half // tile
    held = len(packs) * PACK
    to = lax.broadcasted_iota(jnp.int32, (tiles * held, held * NB), 0)
    source = lax.broadcasted_iota(jnp.int32, (tiles * held, held * NB), 1)
    gather = (source // NB == to % held) & ((source % half) // tile == to // held)
    flat = jnp.dot(
        gather.astype(F32).astype(BF16), jnp.concatenate(spread, axis=0), preferred_element_type=F32
    )
    split = -(-score_rows // 16) * 16
    for seg in range(n):
        rest = [flat[seg % 2 * half_rows + split - score_rows:(seg % 2 + 1) * half_rows]]
        spare = sent_rows - score_rows - half_rows
        if spare:
            rest.append(jnp.zeros((spare, LANES), F32))
        if sent_rows > split:
            out_ref[seg, split:sent_rows, :] = jnp.concatenate(rest, axis=0).astype(BF16)
    to = lax.broadcasted_iota(jnp.int32, (8, held * NB), 0)
    source = lax.broadcasted_iota(jnp.int32, (8, held * NB), 1)
    diagonal = jnp.dot(
        ((source // NB) % 8 == to).astype(F32).astype(BF16), jnp.concatenate(diagonals, axis=0),
        preferred_element_type=F32,
    )
    for c in packs:
        whitening = whitenings[c]
        right = jnp.concatenate(halves(whitening), axis=1)
        for i in range(blocks):
            y = stored[c, i * STEP * n:(i + 1) * STEP * n, :]
            rows_white = nt_dot(jnp.concatenate([y, y], axis=1), right)
            for b in range(STEP):
                w = rows_white[b * n:(b + 1) * n]
                white[c, b, i * n:(i + 1) * n, :] = w.astype(BF16)
                white[c, b, (blocks + i) * n:(blocks + i + 1) * n, :] = up(w).astype(BF16)

    reach = taps + STEP - 1
    fetch_weights.wait()
    fetch_places.wait()
    size = blocks * n
    for c in packs:
        acc = jnp.zeros((size, STEP * rows), F32)
        for u in range(0, reach, 2):
            pair = [u] if u + 1 == reach else [u, u + 1]
            acc = acc + jnp.dot(
                jnp.concatenate(
                    [white[c, v % STEP, (v // STEP) * n:(v // STEP) * n + size, :] for v in pair], axis=1
                ),
                jnp.concatenate(
                    [
                        jnp.concatenate(
                            [weights_ref[c, w * LANES:(w + 1) * LANES, :] for w in (v, v + STEP // 2)], axis=1
                        )
                        for v in pair
                    ],
                    axis=0,
                ),
                preferred_element_type=F32,
            )
        placed = jnp.dot(
            acc.astype(BF16), places_ref[c * STEP * rows:(c + 1) * STEP * rows, :], preferred_element_type=F32
        )
        packed = placed if c == 0 else packed + placed
    for t in range(score_tiles):
        total[t] = packed[:, t * LANES:(t + 1) * LANES]
    for seg in range(n):
        core = seg % 2
        parts = [total[t, pl.ds(seg, blocks, stride=n), :] for t in range(score_tiles)]
        parts[-1] = parts[-1] + diagonal
        if split > score_rows:
            parts.append(flat[core * half_rows:core * half_rows + split - score_rows])
        for t in range(0, len(parts), 2):
            both = jnp.concatenate(parts[t:t + 2], axis=0).astype(BF16)
            out_ref[seg, t * blocks:(t + 2) * blocks, :] = both


def whitening_kernel(groups, width, got_ref, other_ref, turns_ref, whitening_ref, joined):
    n = got_ref.shape[0]
    held = -(-groups // PACK) * PACK
    score_rows, half_rows, sent_rows = layout(groups, width, STEP)
    tiles = half_rows // held
    start = (score_rows - 1) // 16 * 16
    joined[:, 2 * tiles * LANES:] = jnp.zeros((n * groups, LANES), F32)
    for src in range(n):
        rows = slice(src * groups, (src + 1) * groups)
        for ref, place in ((got_ref, 0), (other_ref, 1)):
            block = ref[src, start:sent_rows, :].astype(F32)[score_rows - start:]
            for k in range(tiles):
                at = (place * tiles + k) * LANES
                joined[rows, at:at + LANES] = block[k * held:k * held + groups]
        ends = got_ref[src, start:start + 16, :].astype(F32)[score_rows - STEP - start:]
        for q in range(-(-groups // 8)):
            some = min(8, groups - 8 * q)
            at = (PACK // 2 + q) * NB
            joined[src * groups + 8 * q:src * groups + 8 * q + some, 2 * tiles * LANES:2 * tiles * LANES + NB] = (
                ends[:some, at:at + NB]
            )
    entries = joined[...].astype(BF16)
    step = 2 * LANES
    high = step // NB
    for k in range((NB * NB) // step):
        turned = nt_dot(turns_ref[k * step:(k + 1) * step, :], entries)
        whitening_ref[k * high:(k + 1) * high] = turned.reshape(high, NB, n * groups)


def scores_kernel(groups, per, got_ref, scores_ref, wide):
    length, columns = scores_ref.shape
    blocks = length // STEP
    each = groups * per
    lane = lax.broadcasted_iota(jnp.int32, (blocks, LANES), 1)
    for o in range(columns // LANES):
        for tb in range(STEP):
            out = None
            at = o * LANES
            while at < (o + 1) * LANES:
                src = at // each
                begin = tb * each + at - src * each
                t = begin // LANES
                stop = min((o + 1) * LANES, (src + 1) * each, at + (t + 1) * LANES - begin)
                some = got_ref[src, t // 2 * 16:t // 2 * 16 + 16, :].astype(F32)[t % 2 * 8:t % 2 * 8 + 8]
                shift = (at - begin) % LANES
                moved = pltpu.roll(some, shift, 1) if shift else some
                out = moved if out is None else jnp.where(lane >= at - o * LANES, moved, out)
                at = stop
            wide[o, pl.ds(STEP - 1 - tb, blocks, stride=STEP), :] = out
    for o in range(columns // LANES):
        scores_ref[:, o * LANES:(o + 1) * LANES] = wide[o].astype(BF16)


def params(mib):
    return pltpu.CompilerParams(vmem_limit_bytes=mib * MIB)


def local(raw, pole, order, templates, support):
    length, channels = raw.shape
    n = lax.axis_size("tm")
    me = lax.axis_index("tm").astype(jnp.int32).reshape(1)
    all_groups = channels // NB
    groups = all_groups // n
    per = templates.shape[0] // all_groups
    taps = templates.shape[1]
    count = groups * per
    packs = -(-groups // PACK)
    rows = NB
    width = packs * LANES
    blocks = length // STEP

    if groups % PACK == 0:
        send = raw.reshape(length, n, width).transpose(1, 0, 2)
    else:
        pieces = [raw[:, (d * groups // 2) * 2 * NB:][:, :width] for d in range(n)]
        send = jnp.stack(pieces, axis=0)
    received = lax.all_to_all(send, "tm", 0, 0, tiled=True)

    vmem = pl.BlockSpec(memory_space=pltpu.VMEM)
    anywhere = pl.BlockSpec(memory_space=pl.ANY)
    tap_rows = (taps + 2 * STEP - 2 - (LANES // rows - 1)) * LANES
    by_lane = templates.transpose(1, 2, 0)
    used = support.T
    ends = by_lane.shape[2] // LANES - 1

    def left(s):
        return (s[0] * count) // LANES

    def right(s):
        return jnp.minimum((s[0] * count) // LANES + 1, ends)

    def whole(shape):
        return pl.BlockSpec(shape, lambda i, s: (0,) * len(shape))

    poles = pole.reshape(-1, LANES)
    weights = pl.pallas_call(
        functools.partial(template_kernel, groups, per, rows),
        out_shape=jax.ShapeDtypeStruct((packs, tap_rows, LANES), BF16),
        grid_spec=pltpu.PrefetchScalarGridSpec(
            num_scalar_prefetch=1,
            grid=(1,),
            in_specs=[
                pl.BlockSpec((taps, NB, LANES), lambda i, s: (0, 0, left(s))),
                pl.BlockSpec((taps, NB, LANES), lambda i, s: (0, 0, right(s))),
                pl.BlockSpec((NB, LANES), lambda i, s: (0, left(s))),
                pl.BlockSpec((NB, LANES), lambda i, s: (0, right(s))),
            ],
            out_specs=whole((packs, tap_rows, LANES)),
            scratch_shapes=[pltpu.VMEM(((taps + 2 * STEP - 2) * NB, width), BF16)],
        ),
        compiler_params=params(58),
        name="templates",
    )(me, by_lane, by_lane, used, used)
    score_width = -(-STEP * count // LANES) * LANES
    sent_rows = layout(groups, score_width, blocks)[2]
    picks, permuted, places, turns = pl.pallas_call(
        functools.partial(order_kernel, groups, per, rows),
        out_shape=[
            jax.ShapeDtypeStruct((packs, LANES, LANES), BF16),
            jax.ShapeDtypeStruct((packs, 8, LANES), F32),
            jax.ShapeDtypeStruct((packs * STEP * rows, score_width), BF16),
            jax.ShapeDtypeStruct((NB * NB, NB // 2 * NB + LANES), BF16),
        ],
        in_specs=[pl.BlockSpec(memory_space=pltpu.SMEM), vmem, vmem],
        out_specs=[vmem] * 4,
        compiler_params=params(16),
        name="order",
    )(me, order.T, poles)

    total_rows = n * length
    payload = jax.ShapeDtypeStruct((n, sent_rows, LANES), BF16)
    sent = pl.pallas_call(
        functools.partial(main_kernel, groups, rows, taps),
        out_shape=payload,
        in_specs=[vmem, vmem, vmem, anywhere, anywhere],
        out_specs=vmem,
        scratch_shapes=[
            pltpu.VMEM((packs * STEP * rows, score_width), BF16),
            pltpu.VMEM((packs, tap_rows, LANES), BF16),
            pltpu.VMEM((packs, total_rows, LANES), F32),
            pltpu.VMEM((packs, total_rows, LANES), F32),
            pltpu.VMEM((packs, total_rows, LANES), BF16),
            pltpu.VMEM((packs, STEP, 2 * blocks * n, LANES), BF16),
            pltpu.VMEM((score_width // LANES, blocks * n, LANES), F32),
            pltpu.SemaphoreType.DMA((2,)),
        ],
        compiler_params=params(52),
        name="filter_whiten_match",
    )(received, picks, permuted, places, weights)
    got = lax.all_to_all(sent, "tm", 0, 0, tiled=True)

    other = lax.ppermute(got, "tm", [(i, i ^ 1) for i in range(n)])

    columns = all_groups * per
    scores = pl.pallas_call(
        functools.partial(scores_kernel, groups, per),
        out_shape=jax.ShapeDtypeStruct((length, columns), BF16),
        in_specs=[vmem],
        out_specs=vmem,
        scratch_shapes=[pltpu.VMEM((columns // LANES, length, LANES), F32)],
        cost_estimate=pl.CostEstimate(flops=10**8, bytes_accessed=4 * 10**6, transcendentals=0),
        compiler_params=params(28),
        name="scores",
    )(got)
    whitening = pl.pallas_call(
        functools.partial(whitening_kernel, groups, score_width),
        out_shape=jax.ShapeDtypeStruct((NB, NB, all_groups), F32),
        in_specs=[vmem, vmem, vmem],
        out_specs=vmem,
        scratch_shapes=[pltpu.VMEM((all_groups, NB // 2 * NB + LANES), F32)],
        compiler_params=params(28),
        name="whitening",
    )(got, other, turns)
    return scores, whitening.transpose(2, 0, 1)


def solution(mesh):
    in_specs = (P(("rec", "tm"), None), P(), P(), P(), P())
    out_specs = (P(("rec", "tm"), None), P("rec", None, None))
    return jax.shard_map(local, mesh=mesh, in_specs=in_specs, out_specs=out_specs, check_vma=False)
```

```python
import functools

import jax
import jax.numpy as jnp
from jax import lax
from jax.experimental import pallas as pl
from jax.experimental.pallas import tpu as pltpu
from jax.sharding import PartitionSpec as P

NB = 32
PACK = 4
LANES = NB * PACK
STEP = 8
NS_ITERS = 4
RIDGE = 0.1
MIB = 1024 * 1024
F32, BF16 = jnp.float32, jnp.bfloat16


def nt_dot(a, b):
    return lax.dot_general(a, b, (((1,), (1,)), ((), ())), preferred_element_type=F32)


def halves(a):
    high = a.astype(BF16)
    return high, (a - high.astype(F32)).astype(BF16)


def mul(several, b):
    b_high, b_low = halves(b)
    right = jnp.concatenate([b_high, b_low], axis=1)
    left = [jnp.concatenate(halves(a), axis=1) for a in several]
    out = jnp.dot(
        jnp.concatenate(left, axis=0), jnp.concatenate([right, right], axis=0), preferred_element_type=F32
    )
    out = out[:, :LANES] + out[:, LANES:]
    return [out[k * LANES:(k + 1) * LANES] for k in range(len(several))]


def down(v, distance):
    zeros = jnp.zeros((distance, v.shape[1]), v.dtype)
    return jnp.concatenate([zeros, v[:-distance]], axis=0)


def up(v):
    return jnp.concatenate([v[1:], jnp.zeros((1, v.shape[1]), v.dtype)], axis=0)


def layout(groups, width, blocks):
    score_tiles = width // LANES
    half_rows = (NB // 2 * NB // LANES // 2) * (-(-groups // PACK) * PACK)
    return score_tiles * blocks, half_rows, -(-(score_tiles * blocks + half_rows) // 16) * 16


def template_kernel(
    groups, per, rows, mine, left_ref, right_ref, left_used, right_used, weights_ref, lined
):
    taps = left_ref.shape[0]
    packs = weights_ref.shape[0]
    me = mine[0]
    count = groups * per
    lane = lax.broadcasted_iota(jnp.int32, (2 * LANES, packs * LANES), 1)
    row = lax.broadcasted_iota(jnp.int32, (2 * LANES, packs * LANES), 0)
    number = (lane // LANES) * PACK * per + lane % rows
    real = (lane % rows < PACK * per) & (number < count)
    base = ((me * count) // LANES) * LANES
    select = (real & (base + row == me * count + number)).astype(F32).astype(BF16)
    used = jnp.concatenate([left_used[...], right_used[...]], axis=1).astype(F32).astype(BF16)
    pad = (STEP - 1) * NB
    lined[:pad, :] = jnp.zeros((pad, packs * LANES), BF16)
    lined[pad + taps * NB:, :] = jnp.zeros((pad, packs * LANES), BF16)
    for s in range(0, taps, STEP):
        group = range(s, min(taps, s + STEP))
        blocks = [jnp.concatenate([left_ref[t], right_ref[t]], axis=1) * used for t in group]
        picked = jnp.dot(jnp.concatenate(blocks, axis=0), select, preferred_element_type=F32)
        lined[pad + s * NB:pad + (s + len(group)) * NB, :] = picked.astype(BF16)
    lane = lax.broadcasted_iota(jnp.int32, (NB, LANES), 1)
    taken = [(lane // rows == k).astype(F32).astype(BF16) for k in range(LANES // rows)]
    owned = [((lane % rows) // per == g).astype(F32).astype(BF16) for g in range(PACK)]
    for v in range(weights_ref.shape[1] // LANES):
        for c in range(packs):
            block = sum(
                lined[(v + k) * NB:(v + k + 1) * NB, c * LANES:(c + 1) * LANES] * taken[k]
                for k in range(LANES // rows)
            )
            for g in range(PACK):
                weights_ref[c, v * LANES + g * NB:v * LANES + (g + 1) * NB, :] = block * owned[g]


def order_kernel(groups, per, rows, mine, order_ref, pole_ref, picks_ref, poles_ref, places_ref, turns_ref):
    me = mine[0]
    row = lax.broadcasted_iota(jnp.int32, (places_ref.shape[0], 1), 0)
    number = (row // (STEP * rows)) * PACK * per + row % rows
    held = (row % rows < PACK * per) & (number < groups * per)
    place = jnp.where(held, ((row % (STEP * rows)) // rows) * groups * per + number, -1)
    lane = lax.broadcasted_iota(jnp.int32, places_ref.shape, 1)
    places_ref[...] = (lane == place).astype(F32).astype(BF16)
    row = lax.broadcasted_iota(jnp.int32, (NB * NB, 1), 0)
    low = jnp.minimum(row // NB, row % NB)
    high = jnp.maximum(row // NB, row % NB)
    half = NB // 2
    place = jnp.where(low < high, (high - half) * NB + low - half, half * NB + low)
    place = jnp.where(low < half, low * NB + high, place)
    quarter = half * NB // 2
    swapped = jnp.where(place < quarter, place + quarter, place - quarter)
    place = jnp.where((me % 2 == 1) & (place < half * NB), swapped, place)
    lane = lax.broadcasted_iota(jnp.int32, turns_ref.shape, 1)
    turns_ref[...] = (lane == place).astype(F32).astype(BF16)
    packs = picks_ref.shape[0]
    length, blocks = order_ref.shape
    lane = lax.broadcasted_iota(jnp.int32, (length, blocks), 1)
    ids_lane = lax.broadcasted_iota(jnp.int32, (LANES, LANES), 1)
    for c in range(packs):
        start = me * groups + PACK * c
        block = start // 2
        ids = jnp.concatenate(
            [
                jnp.sum(jnp.where(lane == block + k, order_ref[...], 0), axis=1, keepdims=True) + length * k
                for k in range(2)
            ],
            axis=0,
        )
        pole = pole_ref[pl.ds(block // 2, 1), :]
        if groups % PACK:
            last = pole_ref.shape[0] - 1
            after = pole_ref[pl.ds(jnp.minimum(block // 2 + 1, last), 1), :]
            joined = jnp.concatenate([pole[:, length:], after[:, :length]], axis=1)
            pole = jnp.where(block % 2 == 1, joined, pole)
            ids = jnp.where(start % 2 == 1, jnp.concatenate([ids[NB:], ids[:NB]], axis=0), ids)
        pick = (ids_lane == ids).astype(F32)
        picks_ref[c] = pick.astype(BF16)
        poles_ref[c] = lax.dot_general(
            jnp.broadcast_to(pole, (8, LANES)), pick, (((1,), (1,)), ((), ())),
            precision=lax.Precision.HIGHEST, preferred_element_type=F32,
        )


def main_kernel(
    groups, rows, taps, raw_ref, picks_ref, poles_ref, places_any, weights_any, out_ref,
    places_ref, weights_ref, first, state, stored, white, total, sems,
):
    n, length, width = raw_ref.shape
    fetch_weights = pltpu.make_async_copy(weights_any, weights_ref, sems.at[0])
    fetch_places = pltpu.make_async_copy(places_any, places_ref, sems.at[1])
    packs = range(width // LANES)
    blocks = length // STEP
    pitch = length + 8
    row_id = lax.broadcasted_iota(jnp.int32, (LANES, LANES), 0)
    lane_id = lax.broadcasted_iota(jnp.int32, (LANES, LANES), 1)
    same = (row_id // NB) == (lane_id // NB)
    eye = (row_id == lane_id).astype(F32)
    ones = same.astype(F32).astype(BF16)
    poles = [jnp.broadcast_to(poles_ref[c, :1, :], (n, LANES)) for c in packs]
    gains = [0.5 * (1.0 + pole) for pole in poles]
    fetch_weights.start()
    fetch_places.start()
    for c in packs:
        part = raw_ref[:, :, c * LANES:(c + 1) * LANES].reshape(n * length, LANES)
        picked = nt_dot(part, picks_ref[c])
        for seg in range(n):
            first[c, seg * pitch:seg * pitch + length, :] = picked[seg * length:(seg + 1) * length]

    level = [jnp.zeros((n, LANES), F32) for c in packs]
    last = [down(first[c, pl.ds(length - 1, n, stride=pitch), :], 1) for c in packs]
    for j in range(length):
        for c in packs:
            now = first[c, pl.ds(j, n, stride=pitch), :]
            level[c] = poles[c] * level[c] + gains[c] * (now - last[c])
            last[c] = now
            state[c, j * n:(j + 1) * n, :] = level[c]
    incoming = []
    for c in packs:
        span, square, left = None, poles[c], length
        while left:
            if left % 2:
                span = square if span is None else span * square
            square = square * square
            left //= 2
        value, distance = level[c], 1
        while distance < n:
            value = value + span * down(value, distance)
            span = span * span
            distance *= 2
        incoming.append(down(value, 1))
    carried = list(incoming)
    for j in range(length):
        for c in packs:
            carried[c] = carried[c] * poles[c]
            stored[c, j * n:(j + 1) * n, :] = (state[c, j * n:(j + 1) * n, :] + carried[c]).astype(BF16)

    estimate, inverse, norms = [], [], []
    for c in packs:
        y = stored[c]
        gram = lax.dot_general(y, y, (((0,), (0,)), ((), ())), preferred_element_type=F32)
        cov = jnp.where(same, gram * (1.0 / (n * length)), 0.0)
        sums = jnp.concatenate(
            [jnp.sum(cov * eye, axis=0, keepdims=True), jnp.sum(cov * cov, axis=0, keepdims=True),
             jnp.zeros((6, LANES), F32)], axis=0,
        )
        sums = jnp.dot(jnp.concatenate(halves(sums), axis=0), ones, preferred_element_type=F32)
        sums = sums[:8] + sums[8:]
        trace, squares = sums[0:1], sums[1:2]
        ridge = RIDGE * trace / NB
        norm = jnp.sqrt(squares + 2.0 * ridge * trace + NB * ridge * ridge)
        norms.append(norm)
        estimate.append((cov + ridge * eye) * (1.0 / norm))
    for repeat in range(NS_ITERS):
        if repeat == 0:
            inverse = [1.5 * eye - 0.5 * estimate[c] for c in packs]
            estimate = [mul([estimate[c]], inverse[c])[0] for c in packs]
            continue
        middle = [1.5 * eye - 0.5 * mul([inverse[c]], estimate[c])[0] for c in packs]
        if repeat < NS_ITERS - 1:
            both = [mul([inverse[c], estimate[c]], middle[c]) for c in packs]
            inverse, estimate = [pair[0] for pair in both], [pair[1] for pair in both]
        else:
            inverse = [mul([inverse[c]], middle[c])[0] for c in packs]

    score_tiles = places_ref.shape[1] // LANES
    score_rows, half_rows, sent_rows = layout(groups, places_ref.shape[1], blocks)
    tile, half = LANES // NB, NB // 2
    folded = row_id % NB
    fold = jnp.concatenate([folded == lane_id % NB, folded == lane_id % NB + half], axis=1).astype(F32).astype(BF16)
    j, k = row_id % NB, lane_id % NB
    quarter = lane_id // NB
    spread, diagonals = [], []
    whitenings = [inverse[c] * (1.0 / jnp.sqrt(norms[c])) for c in packs]
    for c in packs:
        wide = jnp.dot(whitenings[c].astype(BF16), fold, preferred_element_type=F32)
        upper = jnp.where((j < half) & (k >= j), wide[:, :LANES], 0.0)
        lower = jnp.where(k < j - half, wide[:, LANES:], 0.0)
        spread.append(jnp.where(quarter == row_id % tile, upper + lower, 0.0).astype(BF16))
        group = c * PACK + row_id // NB
        diagonals.append(
            jnp.where((quarter == tile // 2 + group // 8) & (j == k), wide[:, :LANES], 0.0).astype(BF16)
        )
    tiles = half // tile
    held = len(packs) * PACK
    to = lax.broadcasted_iota(jnp.int32, (tiles * held, held * NB), 0)
    source = lax.broadcasted_iota(jnp.int32, (tiles * held, held * NB), 1)
    gather = (source // NB == to % held) & ((source % half) // tile == to // held)
    flat = jnp.dot(
        gather.astype(F32).astype(BF16), jnp.concatenate(spread, axis=0), preferred_element_type=F32
    )
    split = -(-score_rows // 16) * 16
    for seg in range(n):
        rest = [flat[seg % 2 * half_rows + split - score_rows:(seg % 2 + 1) * half_rows]]
        spare = sent_rows - score_rows - half_rows
        if spare:
            rest.append(jnp.zeros((spare, LANES), F32))
        if sent_rows > split:
            out_ref[seg, split:sent_rows, :] = jnp.concatenate(rest, axis=0).astype(BF16)
    to = lax.broadcasted_iota(jnp.int32, (8, held * NB), 0)
    source = lax.broadcasted_iota(jnp.int32, (8, held * NB), 1)
    diagonal = jnp.dot(
        ((source // NB) % 8 == to).astype(F32).astype(BF16), jnp.concatenate(diagonals, axis=0),
        preferred_element_type=F32,
    )
    for c in packs:
        whitening = whitenings[c]
        right = jnp.concatenate(halves(whitening), axis=1)
        for i in range(blocks):
            y = stored[c, i * STEP * n:(i + 1) * STEP * n, :]
            rows_white = nt_dot(jnp.concatenate([y, y], axis=1), right)
            for b in range(STEP):
                w = rows_white[b * n:(b + 1) * n]
                white[c, b, i * n:(i + 1) * n, :] = w.astype(BF16)
                white[c, b, (blocks + i) * n:(blocks + i + 1) * n, :] = up(w).astype(BF16)

    reach = taps + STEP - 1
    fetch_weights.wait()
    fetch_places.wait()
    size = blocks * n
    for c in packs:
        acc = jnp.zeros((size, STEP * rows), F32)
        for u in range(0, reach, 2):
            pair = [u] if u + 1 == reach else [u, u + 1]
            acc = acc + jnp.dot(
                jnp.concatenate(
                    [white[c, v % STEP, (v // STEP) * n:(v // STEP) * n + size, :] for v in pair], axis=1
                ),
                jnp.concatenate(
                    [
                        jnp.concatenate(
                            [weights_ref[c, w * LANES:(w + 1) * LANES, :] for w in (v, v + STEP // 2)], axis=1
                        )
                        for v in pair
                    ],
                    axis=0,
                ),
                preferred_element_type=F32,
            )
        placed = jnp.dot(
            acc.astype(BF16), places_ref[c * STEP * rows:(c + 1) * STEP * rows, :], preferred_element_type=F32
        )
        packed = placed if c == 0 else packed + placed
    for t in range(score_tiles):
        total[t] = packed[:, t * LANES:(t + 1) * LANES]
    for seg in range(n):
        core = seg % 2
        parts = [total[t, pl.ds(seg, blocks, stride=n), :] for t in range(score_tiles)]
        parts[-1] = parts[-1] + diagonal
        if split > score_rows:
            parts.append(flat[core * half_rows:core * half_rows + split - score_rows])
        for t in range(0, len(parts), 2):
            both = jnp.concatenate(parts[t:t + 2], axis=0).astype(BF16)
            out_ref[seg, t * blocks:(t + 2) * blocks, :] = both


def whitening_kernel(groups, width, got_ref, other_ref, turns_ref, whitening_ref, joined):
    n = got_ref.shape[0]
    held = -(-groups // PACK) * PACK
    score_rows, half_rows, sent_rows = layout(groups, width, STEP)
    tiles = half_rows // held
    start = (score_rows - 1) // 16 * 16
    joined[:, 2 * tiles * LANES:] = jnp.zeros((n * groups, LANES), F32)
    for src in range(n):
        rows = slice(src * groups, (src + 1) * groups)
        for ref, place in ((got_ref, 0), (other_ref, 1)):
            block = ref[src, start:sent_rows, :].astype(F32)[score_rows - start:]
            for k in range(tiles):
                at = (place * tiles + k) * LANES
                joined[rows, at:at + LANES] = block[k * held:k * held + groups]
        ends = got_ref[src, start:start + 16, :].astype(F32)[score_rows - STEP - start:]
        for q in range(-(-groups // 8)):
            some = min(8, groups - 8 * q)
            at = (PACK // 2 + q) * NB
            joined[src * groups + 8 * q:src * groups + 8 * q + some, 2 * tiles * LANES:2 * tiles * LANES + NB] = (
                ends[:some, at:at + NB]
            )
    entries = joined[...].astype(BF16)
    step = 2 * LANES
    high = step // NB
    for k in range((NB * NB) // step):
        turned = nt_dot(turns_ref[k * step:(k + 1) * step, :], entries)
        whitening_ref[k * high:(k + 1) * high] = turned.reshape(high, NB, n * groups)


def scores_kernel(groups, per, got_ref, scores_ref, wide):
    length, columns = scores_ref.shape
    blocks = length // STEP
    each = groups * per
    lane = lax.broadcasted_iota(jnp.int32, (blocks, LANES), 1)
    for o in range(columns // LANES):
        for tb in range(STEP):
            out = None
            at = o * LANES
            while at < (o + 1) * LANES:
                src = at // each
                begin = tb * each + at - src * each
                t = begin // LANES
                stop = min((o + 1) * LANES, (src + 1) * each, at + (t + 1) * LANES - begin)
                some = got_ref[src, t // 2 * 16:t // 2 * 16 + 16, :].astype(F32)[t % 2 * 8:t % 2 * 8 + 8]
                shift = (at - begin) % LANES
                moved = pltpu.roll(some, shift, 1) if shift else some
                out = moved if out is None else jnp.where(lane >= at - o * LANES, moved, out)
                at = stop
            wide[o, pl.ds(STEP - 1 - tb, blocks, stride=STEP), :] = out
    for o in range(columns // LANES):
        scores_ref[:, o * LANES:(o + 1) * LANES] = wide[o].astype(BF16)


def params(mib):
    return pltpu.CompilerParams(vmem_limit_bytes=mib * MIB)


def local(raw, pole, order, templates, support):
    length, channels = raw.shape
    n = lax.axis_size("tm")
    me = lax.axis_index("tm").astype(jnp.int32).reshape(1)
    all_groups = channels // NB
    groups = all_groups // n
    per = templates.shape[0] // all_groups
    taps = templates.shape[1]
    count = groups * per
    packs = -(-groups // PACK)
    rows = NB
    width = packs * LANES
    blocks = length // STEP

    if groups % PACK == 0:
        send = raw.reshape(length, n, width).transpose(1, 0, 2)
    else:
        pieces = [raw[:, (d * groups // 2) * 2 * NB:][:, :width] for d in range(n)]
        send = jnp.stack(pieces, axis=0)
    received = lax.all_to_all(send, "tm", 0, 0, tiled=True)

    vmem = pl.BlockSpec(memory_space=pltpu.VMEM)
    anywhere = pl.BlockSpec(memory_space=pl.ANY)
    tap_rows = (taps + 2 * STEP - 2 - (LANES // rows - 1)) * LANES
    by_lane = templates.transpose(1, 2, 0)
    used = support.T
    ends = by_lane.shape[2] // LANES - 1

    def left(s):
        return (s[0] * count) // LANES

    def right(s):
        return jnp.minimum((s[0] * count) // LANES + 1, ends)

    def whole(shape):
        return pl.BlockSpec(shape, lambda i, s: (0,) * len(shape))

    poles = pole.reshape(-1, LANES)
    weights = pl.pallas_call(
        functools.partial(template_kernel, groups, per, rows),
        out_shape=jax.ShapeDtypeStruct((packs, tap_rows, LANES), BF16),
        grid_spec=pltpu.PrefetchScalarGridSpec(
            num_scalar_prefetch=1,
            grid=(1,),
            in_specs=[
                pl.BlockSpec((taps, NB, LANES), lambda i, s: (0, 0, left(s))),
                pl.BlockSpec((taps, NB, LANES), lambda i, s: (0, 0, right(s))),
                pl.BlockSpec((NB, LANES), lambda i, s: (0, left(s))),
                pl.BlockSpec((NB, LANES), lambda i, s: (0, right(s))),
            ],
            out_specs=whole((packs, tap_rows, LANES)),
            scratch_shapes=[pltpu.VMEM(((taps + 2 * STEP - 2) * NB, width), BF16)],
        ),
        compiler_params=params(58),
        name="templates",
    )(me, by_lane, by_lane, used, used)
    score_width = -(-STEP * count // LANES) * LANES
    sent_rows = layout(groups, score_width, blocks)[2]
    picks, permuted, places, turns = pl.pallas_call(
        functools.partial(order_kernel, groups, per, rows),
        out_shape=[
            jax.ShapeDtypeStruct((packs, LANES, LANES), BF16),
            jax.ShapeDtypeStruct((packs, 8, LANES), F32),
            jax.ShapeDtypeStruct((packs * STEP * rows, score_width), BF16),
            jax.ShapeDtypeStruct((NB * NB, NB // 2 * NB + LANES), BF16),
        ],
        in_specs=[pl.BlockSpec(memory_space=pltpu.SMEM), vmem, vmem],
        out_specs=[vmem] * 4,
        compiler_params=params(16),
        name="order",
    )(me, order.T, poles)

    total_rows = n * length
    payload = jax.ShapeDtypeStruct((n, sent_rows, LANES), BF16)
    sent = pl.pallas_call(
        functools.partial(main_kernel, groups, rows, taps),
        out_shape=payload,
        in_specs=[vmem, vmem, vmem, anywhere, anywhere],
        out_specs=vmem,
        scratch_shapes=[
            pltpu.VMEM((packs * STEP * rows, score_width), BF16),
            pltpu.VMEM((packs, tap_rows, LANES), BF16),
            pltpu.VMEM((packs, total_rows + 8 * n, LANES), F32),
            pltpu.VMEM((packs, total_rows, LANES), F32),
            pltpu.VMEM((packs, total_rows, LANES), BF16),
            pltpu.VMEM((packs, STEP, 2 * blocks * n, LANES), BF16),
            pltpu.VMEM((score_width // LANES, blocks * n, LANES), F32),
            pltpu.SemaphoreType.DMA((2,)),
        ],
        compiler_params=params(52),
        name="filter_whiten_match",
    )(received, picks, permuted, places, weights)
    got = lax.all_to_all(sent, "tm", 0, 0, tiled=True)

    other = lax.ppermute(got, "tm", [(i, i ^ 1) for i in range(n)])

    columns = all_groups * per
    scores = pl.pallas_call(
        functools.partial(scores_kernel, groups, per),
        out_shape=jax.ShapeDtypeStruct((length, columns), BF16),
        in_specs=[vmem],
        out_specs=vmem,
        scratch_shapes=[pltpu.VMEM((columns // LANES, length, LANES), F32)],
        cost_estimate=pl.CostEstimate(flops=10**8, bytes_accessed=4 * 10**6, transcendentals=0),
        compiler_params=params(28),
        name="scores",
    )(got)
    whitening = pl.pallas_call(
        functools.partial(whitening_kernel, groups, score_width),
        out_shape=jax.ShapeDtypeStruct((NB, NB, all_groups), F32),
        in_specs=[vmem, vmem, vmem],
        out_specs=vmem,
        scratch_shapes=[pltpu.VMEM((all_groups, NB // 2 * NB + LANES), F32)],
        compiler_params=params(28),
        name="whitening",
    )(got, other, turns)
    return scores, whitening.transpose(2, 0, 1)


def solution(mesh):
    in_specs = (P(("rec", "tm"), None), P(), P(), P(), P())
    out_specs = (P(("rec", "tm"), None), P("rec", None, None))
    return jax.shard_map(local, mesh=mesh, in_specs=in_specs, out_specs=out_specs, check_vma=False)
```

```python
import functools

import jax
import jax.numpy as jnp
from jax import lax
from jax.experimental import pallas as pl
from jax.experimental.pallas import tpu as pltpu
from jax.sharding import PartitionSpec as P

NB = 32
PACK = 4
LANES = NB * PACK
STEP = 8
NS_ITERS = 4
RIDGE = 0.1
MIB = 1024 * 1024
F32, BF16 = jnp.float32, jnp.bfloat16


def nt_dot(a, b):
    return lax.dot_general(a, b, (((1,), (1,)), ((), ())), preferred_element_type=F32)


def halves(a):
    high = a.astype(BF16)
    return high, (a - high.astype(F32)).astype(BF16)


def mul(several, b):
    b_high, b_low = halves(b)
    right = jnp.concatenate([b_high, b_low], axis=1)
    left = [jnp.concatenate(halves(a), axis=1) for a in several]
    out = jnp.dot(
        jnp.concatenate(left, axis=0), jnp.concatenate([right, right], axis=0), preferred_element_type=F32
    )
    out = out[:, :LANES] + out[:, LANES:]
    return [out[k * LANES:(k + 1) * LANES] for k in range(len(several))]


def down(v, distance):
    zeros = jnp.zeros((distance, v.shape[1]), v.dtype)
    return jnp.concatenate([zeros, v[:-distance]], axis=0)


def up(v):
    return jnp.concatenate([v[1:], jnp.zeros((1, v.shape[1]), v.dtype)], axis=0)


def layout(groups, width, blocks):
    score_tiles = width // LANES
    half_rows = (NB // 2 * NB // LANES // 2) * (-(-groups // PACK) * PACK)
    return score_tiles * blocks, half_rows, -(-(score_tiles * blocks + half_rows) // 16) * 16


def template_kernel(
    groups, per, rows, mine, left_ref, right_ref, left_used, right_used, weights_ref, lined
):
    taps = left_ref.shape[0]
    packs = weights_ref.shape[0]
    me = mine[0]
    count = groups * per
    lane = lax.broadcasted_iota(jnp.int32, (2 * LANES, packs * LANES), 1)
    row = lax.broadcasted_iota(jnp.int32, (2 * LANES, packs * LANES), 0)
    number = (lane // LANES) * PACK * per + lane % rows
    real = (lane % rows < PACK * per) & (number < count)
    base = ((me * count) // LANES) * LANES
    select = (real & (base + row == me * count + number)).astype(F32).astype(BF16)
    used = jnp.concatenate([left_used[...], right_used[...]], axis=1).astype(F32).astype(BF16)
    pad = (STEP - 1) * NB
    lined[:pad, :] = jnp.zeros((pad, packs * LANES), BF16)
    lined[pad + taps * NB:, :] = jnp.zeros((pad, packs * LANES), BF16)
    for s in range(0, taps, STEP):
        group = range(s, min(taps, s + STEP))
        blocks = [jnp.concatenate([left_ref[t], right_ref[t]], axis=1) * used for t in group]
        picked = jnp.dot(jnp.concatenate(blocks, axis=0), select, preferred_element_type=F32)
        lined[pad + s * NB:pad + (s + len(group)) * NB, :] = picked.astype(BF16)
    lane = lax.broadcasted_iota(jnp.int32, (NB, LANES), 1)
    taken = [(lane // rows == k).astype(F32).astype(BF16) for k in range(LANES // rows)]
    owned = [((lane % rows) // per == g).astype(F32).astype(BF16) for g in range(PACK)]
    for v in range(weights_ref.shape[1] // LANES):
        for c in range(packs):
            block = sum(
                lined[(v + k) * NB:(v + k + 1) * NB, c * LANES:(c + 1) * LANES] * taken[k]
                for k in range(LANES // rows)
            )
            for g in range(PACK):
                weights_ref[c, v * LANES + g * NB:v * LANES + (g + 1) * NB, :] = block * owned[g]


def order_kernel(groups, per, rows, mine, order_ref, pole_ref, picks_ref, poles_ref, places_ref, turns_ref):
    me = mine[0]
    row = lax.broadcasted_iota(jnp.int32, (places_ref.shape[0], 1), 0)
    number = (row // (STEP * rows)) * PACK * per + row % rows
    held = (row % rows < PACK * per) & (number < groups * per)
    place = jnp.where(held, ((row % (STEP * rows)) // rows) * groups * per + number, -1)
    lane = lax.broadcasted_iota(jnp.int32, places_ref.shape, 1)
    places_ref[...] = (lane == place).astype(F32).astype(BF16)
    row = lax.broadcasted_iota(jnp.int32, (NB * NB, 1), 0)
    low = jnp.minimum(row // NB, row % NB)
    high = jnp.maximum(row // NB, row % NB)
    half = NB // 2
    place = jnp.where(low < high, (high - half) * NB + low - half, half * NB + low)
    place = jnp.where(low < half, low * NB + high, place)
    quarter = half * NB // 2
    swapped = jnp.where(place < quarter, place + quarter, place - quarter)
    place = jnp.where((me % 2 == 1) & (place < half * NB), swapped, place)
    lane = lax.broadcasted_iota(jnp.int32, turns_ref.shape, 1)
    turns_ref[...] = (lane == place).astype(F32).astype(BF16)
    packs = picks_ref.shape[0]
    length, blocks = order_ref.shape
    lane = lax.broadcasted_iota(jnp.int32, (length, blocks), 1)
    ids_lane = lax.broadcasted_iota(jnp.int32, (LANES, LANES), 1)
    for c in range(packs):
        start = me * groups + PACK * c
        block = start // 2
        ids = jnp.concatenate(
            [
                jnp.sum(jnp.where(lane == block + k, order_ref[...], 0), axis=1, keepdims=True) + length * k
                for k in range(2)
            ],
            axis=0,
        )
        pole = pole_ref[pl.ds(block // 2, 1), :]
        if groups % PACK:
            last = pole_ref.shape[0] - 1
            after = pole_ref[pl.ds(jnp.minimum(block // 2 + 1, last), 1), :]
            joined = jnp.concatenate([pole[:, length:], after[:, :length]], axis=1)
            pole = jnp.where(block % 2 == 1, joined, pole)
            ids = jnp.where(start % 2 == 1, jnp.concatenate([ids[NB:], ids[:NB]], axis=0), ids)
        pick = (ids_lane == ids).astype(F32)
        picks_ref[c] = pick.astype(BF16)
        poles_ref[c] = lax.dot_general(
            jnp.broadcast_to(pole, (8, LANES)), pick, (((1,), (1,)), ((), ())),
            precision=lax.Precision.HIGHEST, preferred_element_type=F32,
        )


def main_kernel(
    groups, rows, taps, raw_ref, picks_ref, poles_ref, places_any, weights_any, out_ref,
    places_ref, weights_ref, first, state, stored, white, total, sems,
):
    n, length, width = raw_ref.shape
    fetch_weights = pltpu.make_async_copy(weights_any, weights_ref, sems.at[0])
    fetch_places = pltpu.make_async_copy(places_any, places_ref, sems.at[1])
    packs = range(width // LANES)
    blocks = length // STEP
    pitch = length + 8
    row_id = lax.broadcasted_iota(jnp.int32, (LANES, LANES), 0)
    lane_id = lax.broadcasted_iota(jnp.int32, (LANES, LANES), 1)
    same = (row_id // NB) == (lane_id // NB)
    eye = (row_id == lane_id).astype(F32)
    ones = same.astype(F32).astype(BF16)
    poles = [jnp.broadcast_to(poles_ref[c, :1, :], (n, LANES)) for c in packs]
    gains = [0.5 * (1.0 + pole) for pole in poles]
    fetch_weights.start()
    fetch_places.start()
    for c in packs:
        part = raw_ref[:, :, c * LANES:(c + 1) * LANES].reshape(n * length, LANES)
        picked = nt_dot(part, picks_ref[c])
        for seg in range(n):
            first[c, seg * pitch:seg * pitch + length, :] = picked[seg * length:(seg + 1) * length]

    level = [jnp.zeros((n, LANES), F32) for c in packs]
    last = [down(first[c, pl.ds(length - 1, n, stride=pitch), :], 1) for c in packs]
    for j in range(length):
        for c in packs:
            now = first[c, pl.ds(j, n, stride=pitch), :]
            level[c] = poles[c] * level[c] + gains[c] * (now - last[c])
            last[c] = now
            state[c, j * n:(j + 1) * n, :] = level[c]
    incoming = []
    for c in packs:
        span, square, left = None, poles[c], length
        while left:
            if left % 2:
                span = square if span is None else span * square
            square = square * square
            left //= 2
        value, distance = level[c], 1
        while distance < n:
            value = value + span * down(value, distance)
            span = span * span
            distance *= 2
        incoming.append(down(value, 1))
    carried = list(incoming)
    for j in range(length):
        for c in packs:
            carried[c] = carried[c] * poles[c]
            stored[c, j * n:(j + 1) * n, :] = (state[c, j * n:(j + 1) * n, :] + carried[c]).astype(BF16)

    estimate, inverse, norms = [], [], []
    for c in packs:
        y = stored[c]
        gram = lax.dot_general(y, y, (((0,), (0,)), ((), ())), preferred_element_type=F32)
        cov = jnp.where(same, gram * (1.0 / (n * length)), 0.0)
        sums = jnp.concatenate(
            [jnp.sum(cov * eye, axis=0, keepdims=True), jnp.sum(cov * cov, axis=0, keepdims=True),
             jnp.zeros((6, LANES), F32)], axis=0,
        )
        sums = jnp.dot(jnp.concatenate(halves(sums), axis=0), ones, preferred_element_type=F32)
        sums = sums[:8] + sums[8:]
        trace, squares = sums[0:1], sums[1:2]
        ridge = RIDGE * trace / NB
        norm = jnp.sqrt(squares + 2.0 * ridge * trace + NB * ridge * ridge)
        norms.append(norm)
        estimate.append((cov + ridge * eye) * (1.0 / norm))
    for repeat in range(NS_ITERS):
        if repeat == 0:
            inverse = [1.5 * eye - 0.5 * estimate[c] for c in packs]
            estimate = [mul([estimate[c]], inverse[c])[0] for c in packs]
            continue
        middle = [1.5 * eye - 0.5 * mul([inverse[c]], estimate[c])[0] for c in packs]
        if repeat < NS_ITERS - 1:
            both = [mul([inverse[c], estimate[c]], middle[c]) for c in packs]
            inverse, estimate = [pair[0] for pair in both], [pair[1] for pair in both]
        else:
            inverse = [mul([inverse[c]], middle[c])[0] for c in packs]

    score_tiles = places_ref.shape[1] // LANES
    score_rows, half_rows, sent_rows = layout(groups, places_ref.shape[1], blocks)
    tile, half = LANES // NB, NB // 2
    folded = row_id % NB
    fold = jnp.concatenate([folded == lane_id % NB, folded == lane_id % NB + half], axis=1).astype(F32).astype(BF16)
    j, k = row_id % NB, lane_id % NB
    quarter = lane_id // NB
    spread, diagonals = [], []
    whitenings = [inverse[c] * (1.0 / jnp.sqrt(norms[c])) for c in packs]
    for c in packs:
        wide = jnp.dot(whitenings[c].astype(BF16), fold, preferred_element_type=F32)
        upper = jnp.where((j < half) & (k >= j), wide[:, :LANES], 0.0)
        lower = jnp.where(k < j - half, wide[:, LANES:], 0.0)
        spread.append(jnp.where(quarter == row_id % tile, upper + lower, 0.0).astype(BF16))
        group = c * PACK + row_id // NB
        diagonals.append(
            jnp.where((quarter == tile // 2 + group // 8) & (j == k), wide[:, :LANES], 0.0).astype(BF16)
        )
    tiles = half // tile
    held = len(packs) * PACK
    to = lax.broadcasted_iota(jnp.int32, (tiles * held, held * NB), 0)
    source = lax.broadcasted_iota(jnp.int32, (tiles * held, held * NB), 1)
    gather = (source // NB == to % held) & ((source % half) // tile == to // held)
    flat = jnp.dot(
        gather.astype(F32).astype(BF16), jnp.concatenate(spread, axis=0), preferred_element_type=F32
    )
    split = -(-score_rows // 16) * 16
    for seg in range(n):
        rest = [flat[seg % 2 * half_rows + split - score_rows:(seg % 2 + 1) * half_rows]]
        spare = sent_rows - score_rows - half_rows
        if spare:
            rest.append(jnp.zeros((spare, LANES), F32))
        if sent_rows > split:
            out_ref[seg, split:sent_rows, :] = jnp.concatenate(rest, axis=0).astype(BF16)
    to = lax.broadcasted_iota(jnp.int32, (8, held * NB), 0)
    source = lax.broadcasted_iota(jnp.int32, (8, held * NB), 1)
    diagonal = jnp.dot(
        ((source // NB) % 8 == to).astype(F32).astype(BF16), jnp.concatenate(diagonals, axis=0),
        preferred_element_type=F32,
    )
    for c in packs:
        whitening = whitenings[c]
        right = jnp.concatenate(halves(whitening), axis=1)
        for i in range(blocks):
            y = stored[c, i * STEP * n:(i + 1) * STEP * n, :]
            rows_white = nt_dot(jnp.concatenate([y, y], axis=1), right)
            for b in range(STEP):
                w = rows_white[b * n:(b + 1) * n]
                white[c, b, i * n:(i + 1) * n, :] = w.astype(BF16)
                white[c, b, (blocks + i) * n:(blocks + i + 1) * n, :] = up(w).astype(BF16)

    reach = taps + STEP - 1
    fetch_weights.wait()
    fetch_places.wait()
    size = blocks * n
    for c in packs:
        acc = jnp.zeros((size, STEP * rows), F32)
        for u in range(0, reach, 2):
            pair = [u] if u + 1 == reach else [u, u + 1]
            acc = acc + jnp.dot(
                jnp.concatenate(
                    [white[c, v % STEP, (v // STEP) * n:(v // STEP) * n + size, :] for v in pair], axis=1
                ),
                jnp.concatenate(
                    [
                        jnp.concatenate(
                            [weights_ref[c, w * LANES:(w + 1) * LANES, :] for w in (v, v + STEP // 2)], axis=1
                        )
                        for v in pair
                    ],
                    axis=0,
                ),
                preferred_element_type=F32,
            )
        placed = jnp.dot(
            acc.astype(BF16), places_ref[c * STEP * rows:(c + 1) * STEP * rows, :], preferred_element_type=F32
        )
        packed = placed if c == 0 else packed + placed
    apart = n + 8
    for t in range(score_tiles):
        for i in range(blocks):
            total[t, i * apart:i * apart + n, :] = packed[i * n:(i + 1) * n, t * LANES:(t + 1) * LANES]
    for seg in range(n):
        core = seg % 2
        parts = [total[t, pl.ds(seg, blocks, stride=apart), :] for t in range(score_tiles)]
        parts[-1] = parts[-1] + diagonal
        if split > score_rows:
            parts.append(flat[core * half_rows:core * half_rows + split - score_rows])
        for t in range(0, len(parts), 2):
            both = jnp.concatenate(parts[t:t + 2], axis=0).astype(BF16)
            out_ref[seg, t * blocks:(t + 2) * blocks, :] = both


def whitening_kernel(groups, width, got_ref, other_ref, turns_ref, whitening_ref, joined):
    n = got_ref.shape[0]
    held = -(-groups // PACK) * PACK
    score_rows, half_rows, sent_rows = layout(groups, width, STEP)
    tiles = half_rows // held
    start = (score_rows - 1) // 16 * 16
    joined[:, 2 * tiles * LANES:] = jnp.zeros((n * groups, LANES), F32)
    for src in range(n):
        rows = slice(src * groups, (src + 1) * groups)
        for ref, place in ((got_ref, 0), (other_ref, 1)):
            block = ref[src, start:sent_rows, :].astype(F32)[score_rows - start:]
            for k in range(tiles):
                at = (place * tiles + k) * LANES
                joined[rows, at:at + LANES] = block[k * held:k * held + groups]
        ends = got_ref[src, start:start + 16, :].astype(F32)[score_rows - STEP - start:]
        for q in range(-(-groups // 8)):
            some = min(8, groups - 8 * q)
            at = (PACK // 2 + q) * NB
            joined[src * groups + 8 * q:src * groups + 8 * q + some, 2 * tiles * LANES:2 * tiles * LANES + NB] = (
                ends[:some, at:at + NB]
            )
    entries = joined[...].astype(BF16)
    step = 2 * LANES
    high = step // NB
    for k in range((NB * NB) // step):
        turned = nt_dot(turns_ref[k * step:(k + 1) * step, :], entries)
        whitening_ref[k * high:(k + 1) * high] = turned.reshape(high, NB, n * groups)


def scores_kernel(groups, per, got_ref, scores_ref, wide):
    length, columns = scores_ref.shape
    blocks = length // STEP
    each = groups * per
    lane = lax.broadcasted_iota(jnp.int32, (blocks, LANES), 1)
    for o in range(columns // LANES):
        for tb in range(STEP):
            out = None
            at = o * LANES
            while at < (o + 1) * LANES:
                src = at // each
                begin = tb * each + at - src * each
                t = begin // LANES
                stop = min((o + 1) * LANES, (src + 1) * each, at + (t + 1) * LANES - begin)
                some = got_ref[src, t // 2 * 16:t // 2 * 16 + 16, :].astype(F32)[t % 2 * 8:t % 2 * 8 + 8]
                shift = (at - begin) % LANES
                moved = pltpu.roll(some, shift, 1) if shift else some
                out = moved if out is None else jnp.where(lane >= at - o * LANES, moved, out)
                at = stop
            wide[o, pl.ds(STEP - 1 - tb, blocks, stride=STEP), :] = out
    for o in range(columns // LANES):
        scores_ref[:, o * LANES:(o + 1) * LANES] = wide[o].astype(BF16)


def params(mib):
    return pltpu.CompilerParams(vmem_limit_bytes=mib * MIB)


def local(raw, pole, order, templates, support):
    length, channels = raw.shape
    n = lax.axis_size("tm")
    me = lax.axis_index("tm").astype(jnp.int32).reshape(1)
    all_groups = channels // NB
    groups = all_groups // n
    per = templates.shape[0] // all_groups
    taps = templates.shape[1]
    count = groups * per
    packs = -(-groups // PACK)
    rows = NB
    width = packs * LANES
    blocks = length // STEP

    if groups % PACK == 0:
        send = raw.reshape(length, n, width).transpose(1, 0, 2)
    else:
        pieces = [raw[:, (d * groups // 2) * 2 * NB:][:, :width] for d in range(n)]
        send = jnp.stack(pieces, axis=0)
    received = lax.all_to_all(send, "tm", 0, 0, tiled=True)

    vmem = pl.BlockSpec(memory_space=pltpu.VMEM)
    anywhere = pl.BlockSpec(memory_space=pl.ANY)
    tap_rows = (taps + 2 * STEP - 2 - (LANES // rows - 1)) * LANES
    by_lane = templates.transpose(1, 2, 0)
    used = support.T
    ends = by_lane.shape[2] // LANES - 1

    def left(s):
        return (s[0] * count) // LANES

    def right(s):
        return jnp.minimum((s[0] * count) // LANES + 1, ends)

    def whole(shape):
        return pl.BlockSpec(shape, lambda i, s: (0,) * len(shape))

    poles = pole.reshape(-1, LANES)
    weights = pl.pallas_call(
        functools.partial(template_kernel, groups, per, rows),
        out_shape=jax.ShapeDtypeStruct((packs, tap_rows, LANES), BF16),
        grid_spec=pltpu.PrefetchScalarGridSpec(
            num_scalar_prefetch=1,
            grid=(1,),
            in_specs=[
                pl.BlockSpec((taps, NB, LANES), lambda i, s: (0, 0, left(s))),
                pl.BlockSpec((taps, NB, LANES), lambda i, s: (0, 0, right(s))),
                pl.BlockSpec((NB, LANES), lambda i, s: (0, left(s))),
                pl.BlockSpec((NB, LANES), lambda i, s: (0, right(s))),
            ],
            out_specs=whole((packs, tap_rows, LANES)),
            scratch_shapes=[pltpu.VMEM(((taps + 2 * STEP - 2) * NB, width), BF16)],
        ),
        compiler_params=params(58),
        name="templates",
    )(me, by_lane, by_lane, used, used)
    score_width = -(-STEP * count // LANES) * LANES
    sent_rows = layout(groups, score_width, blocks)[2]
    picks, permuted, places, turns = pl.pallas_call(
        functools.partial(order_kernel, groups, per, rows),
        out_shape=[
            jax.ShapeDtypeStruct((packs, LANES, LANES), BF16),
            jax.ShapeDtypeStruct((packs, 8, LANES), F32),
            jax.ShapeDtypeStruct((packs * STEP * rows, score_width), BF16),
            jax.ShapeDtypeStruct((NB * NB, NB // 2 * NB + LANES), BF16),
        ],
        in_specs=[pl.BlockSpec(memory_space=pltpu.SMEM), vmem, vmem],
        out_specs=[vmem] * 4,
        compiler_params=params(16),
        name="order",
    )(me, order.T, poles)

    total_rows = n * length
    payload = jax.ShapeDtypeStruct((n, sent_rows, LANES), BF16)
    sent = pl.pallas_call(
        functools.partial(main_kernel, groups, rows, taps),
        out_shape=payload,
        in_specs=[vmem, vmem, vmem, anywhere, anywhere],
        out_specs=vmem,
        scratch_shapes=[
            pltpu.VMEM((packs * STEP * rows, score_width), BF16),
            pltpu.VMEM((packs, tap_rows, LANES), BF16),
            pltpu.VMEM((packs, total_rows + 8 * n, LANES), F32),
            pltpu.VMEM((packs, total_rows, LANES), F32),
            pltpu.VMEM((packs, total_rows, LANES), BF16),
            pltpu.VMEM((packs, STEP, 2 * blocks * n, LANES), BF16),
            pltpu.VMEM((score_width // LANES, blocks * (n + 8), LANES), F32),
            pltpu.SemaphoreType.DMA((2,)),
        ],
        compiler_params=params(52),
        name="filter_whiten_match",
    )(received, picks, permuted, places, weights)
    got = lax.all_to_all(sent, "tm", 0, 0, tiled=True)

    other = lax.ppermute(got, "tm", [(i, i ^ 1) for i in range(n)])

    columns = all_groups * per
    scores = pl.pallas_call(
        functools.partial(scores_kernel, groups, per),
        out_shape=jax.ShapeDtypeStruct((length, columns), BF16),
        in_specs=[vmem],
        out_specs=vmem,
        scratch_shapes=[pltpu.VMEM((columns // LANES, length, LANES), F32)],
        cost_estimate=pl.CostEstimate(flops=10**8, bytes_accessed=4 * 10**6, transcendentals=0),
        compiler_params=params(28),
        name="scores",
    )(got)
    whitening = pl.pallas_call(
        functools.partial(whitening_kernel, groups, score_width),
        out_shape=jax.ShapeDtypeStruct((NB, NB, all_groups), F32),
        in_specs=[vmem, vmem, vmem],
        out_specs=vmem,
        scratch_shapes=[pltpu.VMEM((all_groups, NB // 2 * NB + LANES), F32)],
        compiler_params=params(28),
        name="whitening",
    )(got, other, turns)
    return scores, whitening.transpose(2, 0, 1)


def solution(mesh):
    in_specs = (P(("rec", "tm"), None), P(), P(), P(), P())
    out_specs = (P(("rec", "tm"), None), P("rec", None, None))
    return jax.shard_map(local, mesh=mesh, in_specs=in_specs, out_specs=out_specs, check_vma=False)
```
